256 devices in a mesh: brick: 32 (over z_hi, x, core), view: 8 (over y, z_lo).
Axes of the slice: x: 4, y: 4, z: 8 (z_hi: 4, z_lo: 2; z = z_hi * 2 + z_lo), core: 2. Of those that a mesh axis runs over, the one named last changes fastest.
Arguments:
- estimate: float32 [256, 64, 512], P('brick'), may hold values from 0.5 to 2
- camera_blocks: bfloat16 [8, 512, 8, 2048], P('view', 'brick'), may hold values from 0.099609375 to 2
- block_lists: int32 [8, 32, 32, 2], P('view'), may hold values from -1 to 15, as said below
- block_offsets: int32 [8, 512], P('view'), may hold values from 1 to 252, as said below
- psf_index: int32 [8, 64], P('view'), may hold values from 0 to 15
- psf_bank: float32 [8, 2, 16, 9], P('view'), may hold values from 0.03 to 0.3
Outputs:
- updated: float32 [256, 64, 512], P('brick')
The draws below stay inside these ranges and needn't reach their ends.
Inputs may be any that keep to these rules, and one draw needn't show every extreme that they name: block_lists[v, d, s] names exactly the blocks of holder s that intersect brick d, each once; at most 2 of them, and 2 for some brick and holder. `block_offsets`: every block starts after its brick's first row by 1 to 4 rows.
All inputs are finite; a program needn't handle non-finite values.
Results may differ from the reference program's by a relative error of at most 0.0003.
Values may be sent and summed in bfloat16 or wider, within the bound.
A program may use at most 128 MiB of HBM per device.

```python
import math
import jax
import jax.numpy as jnp
from jax import lax

VIEWS = 8
X_DEV = 8
NX = 256
NZ = 64
NY = 512
TY = 32
TILES_DEV = 16
CAP = 2
NKERN = 16
TAPS = 9


def layout_tables(key):
    brick_count = NX // X_DEV
    radius = TAPS // 2

    def one_view(view_key):
        key_first, key_rest, key_jit = jax.random.split(view_key, 3)
        first_shift = jax.random.randint(key_first, (), 0, brick_count).astype(jnp.int32)
        others = jax.random.permutation(key_rest, brick_count - 2)[:TILES_DEV - 2].astype(jnp.int32)
        shifts = jnp.concatenate([jnp.stack([first_shift, (first_shift + 1) % brick_count]), (first_shift + 2 + others) % brick_count]).astype(jnp.int32)
        jitter = jax.random.randint(key_jit, (brick_count, TILES_DEV), 1, radius + 1).astype(jnp.int32)
        low_source = (brick_count - shifts[0]) % brick_count
        high_source = (brick_count - 1 - shifts[0]) % brick_count
        jitter = jitter.at[high_source, 0].set(radius).at[low_source, 0].set(1)
        source_ids = jnp.arange(brick_count, dtype=jnp.int32)
        x_rows = (source_ids[:, None] + shifts[None, :]) % brick_count
        offsets = (x_rows * X_DEV + jitter).reshape(-1)
        dest_ids = source_ids[:, None, None]
        block_ids = jnp.arange(TILES_DEV, dtype=jnp.int32)[None, None, :]
        same_row = x_rows[None, :, :] == dest_ids
        row_before = x_rows[None, :, :] == dest_ids - 1
        own_block = jnp.where(jnp.any(same_row, axis=2), jnp.sum(jnp.where(same_row, block_ids, 0), axis=2), -1)
        before = jnp.where(jnp.any(row_before, axis=2), jnp.sum(jnp.where(row_before, block_ids, 0), axis=2), -1)
        tables = jnp.stack([own_block, before], axis=-1)
        return (tables.astype(jnp.int32), offsets.astype(jnp.int32))
    return jax.vmap(one_view)(jax.random.split(key, VIEWS))


def draw_block_lists(key, part):
    return layout_tables(jax.random.fold_in(key, 17))[0]


def draw_block_offsets(key, part):
    return layout_tables(jax.random.fold_in(key, 17))[1]


def plant(values, key, smallest, top_value):
    longest = values.shape.index(max(values.shape))
    spots = []
    for shift in (0, 1):
        where = [jax.random.randint(jax.random.fold_in(key, axis), (), 0, length) for axis, length in enumerate(values.shape)]
        where[longest] = (where[longest] + shift) % values.shape[longest]
        spots.append(tuple(where))
    return values.at[spots[0]].set(smallest).at[spots[1]].set(top_value)


def shard_levels(stream_key, shape, cuts, smallest, high):
    level = 1.0
    for dim, parts in cuts:
        heights = jax.random.uniform(jax.random.fold_in(jax.random.fold_in(stream_key, 6), dim), (parts,), jnp.float32, smallest / len(cuts), high / len(cuts))
        level = level * jnp.repeat(jnp.exp(heights), shape[dim] // parts).reshape((-1,) + (1,) * (len(shape) - 1 - dim))
    return level


def setup_inputs(seed: int = 0) -> dict:
    streams_of = jax.random.split(jax.random.key(seed), 7)
    estimate = jnp.clip(0.5 + 1.5 * jax.random.uniform(streams_of[0], (NX, NZ, NY), jnp.float32) ** shard_levels(streams_of[0], (NX, NZ, NY), ((0, 32),), -0.2, 0.2), 0.5, 2.0)
    camera_blocks = jnp.clip(jnp.exp(math.log(2.0) - 2.9996462 * jax.random.uniform(streams_of[1], (VIEWS, NX // X_DEV * TILES_DEV, X_DEV, NZ * TY), jnp.float32) ** shard_levels(streams_of[1], (VIEWS, NX // X_DEV * TILES_DEV, X_DEV, NZ * TY), ((0, 8), (1, 32)), -0.2, 0.2)), 0.099609375, 2.0).astype(jnp.bfloat16)
    block_lists = draw_block_lists(jax.random.fold_in(streams_of[6], 71), 0)
    block_offsets = draw_block_offsets(jax.random.fold_in(streams_of[6], 71), 0)
    psf_index = plant(jax.random.randint(streams_of[4], (VIEWS, NZ), 0, NKERN), jax.random.fold_in(streams_of[4], 1), 0, NKERN - 1).astype(jnp.int32)
    psf_bank = jnp.clip(jnp.exp(math.log(0.3) - 2.3025852 * jax.random.uniform(streams_of[5], (VIEWS, 2, NKERN, TAPS), jnp.float32) ** shard_levels(streams_of[5], (VIEWS, 2, NKERN, TAPS), ((0, 8),), -0.2, 0.2)), 0.03, 0.3)
    return {"estimate": estimate, "camera_blocks": camera_blocks, "block_lists": block_lists, "block_offsets": block_offsets, "psf_index": psf_index, "psf_bank": psf_bank}


def blur_cols(field, kern, reverse):
    tap_count = kern.shape[1]
    radius = tap_count // 2
    width = field.shape[2]
    padded = jnp.pad(field, ((0, 0), (0, 0), (radius, radius)))
    result = None
    for offset in range(tap_count):
        begin_at = 2 * radius - offset if reverse else offset
        term = kern[:, offset][None, :, None] * padded[:, :, begin_at:begin_at + width]
        result = term if result is None else result + term
    return result


def blur_rows(padded, kern, reverse, rows):
    tap_count = kern.shape[1]
    radius = tap_count // 2
    result = None
    for offset in range(tap_count):
        begin_at = 2 * radius - offset if reverse else offset
        term = kern[:, offset][None, :, None] * padded[begin_at:begin_at + rows]
        result = term if result is None else result + term
    return result


def assemble(blocks_view, lists_view, offsets_view):
    brick_count = NX // X_DEV
    canvas = jnp.zeros((NX + 2 * X_DEV, NZ, NY), jnp.float32)

    def place_one(index, canvas):
        index = jnp.asarray(index).astype(jnp.int32)
        dest_id = index // (brick_count * CAP)
        source_id = (index // CAP) % brick_count
        slot_id = index % CAP
        block_id = lists_view[dest_id, source_id, slot_id].astype(jnp.int32)
        is_valid = block_id >= 0
        safe_id = jnp.maximum(block_id, 0).astype(jnp.int32)
        global_id = (source_id * TILES_DEV + safe_id).astype(jnp.int32)
        block_data = lax.dynamic_index_in_dim(blocks_view, global_id, 0, keepdims=False)
        block_data = block_data.astype(jnp.float32).reshape(X_DEV, NZ, TY)
        row_start = offsets_view[global_id].astype(jnp.int32)
        row_ids = row_start + jnp.arange(X_DEV).astype(jnp.int32)
        row_keep = (row_ids >= dest_id * X_DEV) & (row_ids < (dest_id + 1) * X_DEV) & is_valid
        block_data = block_data * row_keep[:, None, None].astype(jnp.float32)
        corner = ((row_start + X_DEV).astype(jnp.int32), jnp.zeros((), jnp.int32), (safe_id * TY).astype(jnp.int32))
        previous = lax.dynamic_slice(canvas, corner, block_data.shape)
        return lax.dynamic_update_slice(canvas, previous + block_data, corner)

    canvas = lax.fori_loop(0, brick_count * brick_count * CAP, place_one, canvas)
    return canvas[X_DEV:X_DEV + NX]


def reference(estimate, camera_blocks, block_lists, block_offsets, psf_index, psf_bank):
    radius = TAPS // 2
    product = None
    for view_id in range(VIEWS):
        kern_x = psf_bank[view_id, 0][psf_index[view_id]]
        kern_y = psf_bank[view_id, 1][psf_index[view_id]]
        measured = assemble(camera_blocks[view_id], block_lists[view_id], block_offsets[view_id])
        padded = jnp.pad(estimate, ((radius, radius), (0, 0), (0, 0)))
        blurred = blur_rows(blur_cols(padded, kern_y, False), kern_x, False, NX)
        ratio = measured / blurred
        padded_ratio = jnp.pad(ratio, ((radius, radius), (0, 0), (0, 0)))
        correction = blur_rows(blur_cols(padded_ratio, kern_y, True), kern_x, True, NX)
        product = correction if product is None else product * correction
    return estimate * product
```

```python
import functools

import jax
import jax.numpy as jnp
from jax import lax
from jax.experimental import pallas as pl
from jax.experimental.pallas import tpu as pltpu
from jax.sharding import PartitionSpec as P

F32 = jnp.float32
BF16 = jnp.bfloat16
MESH = pl.DeviceIdType.MESH
TAPS = 9
RAD = TAPS // 2
ROWS = 256
GROUPS = 4
PAD = 8
META = 56


def column_pass(parts, tap, reverse):
    lane = lax.broadcasted_iota(jnp.int32, (8, 128), 1)
    sums = [tap(RAD) * part for part in parts]
    for shift in range(-RAD, RAD + 1):
        if shift == 0:
            continue
        weight = tap(RAD - shift if reverse else RAD + shift)
        turned = [pltpu.roll(part, (-shift) % 128, 1) for part in parts]
        keep = lane < 128 - shift if shift > 0 else lane >= -shift
        for g in range(GROUPS):
            other = g + 1 if shift > 0 else g - 1
            beside = turned[other] if 0 <= other < GROUPS else jnp.zeros((8, 128), F32)
            sums[g] = sums[g] + weight * jnp.where(keep, turned[g], beside)
    return sums


def row_pass(load, tap, reverse):
    total = None
    for shift in range(-RAD, RAD + 1):
        weight = tap(RAD - shift if reverse else RAD + shift)
        term = weight * load(shift)
        total = term if total is None else total + term
    return total


def swap_lanes(low, high, width, keep):
    new_low = jnp.where(keep, low, pltpu.roll(high, width, 1))
    new_high = jnp.where(keep, pltpu.roll(low, 128 - width, 1), high)
    return new_low, new_high


def kernel(
    est_ref, cam_ref, table_ref, index_ref, bank_ref, out_ref,
    cam_t, cam_r, est_t, est_r, meta_s, meta_r, taps, onehot, blurred, ratio, part, other, back,
    s_est, r_est, s_fwd, r_fwd, s_meta, r_meta, s_cam, r_cam, s_half, r_half, s_back, r_back, s_out, r_out,
):
    brick = lax.axis_index("brick")
    view = lax.axis_index("view")
    zh, x, c = brick // 8, (brick // 2) % 4, brick % 2
    y, zl = view // 2, view % 2
    core_of_y = y // 2
    half_of_zh = zh // 2

    def place(zh_, x_, c_, y_, zl_):
        return (zh_ * 8 + x_ * 2 + c_, y_ * 2 + zl_)

    barrier = pltpu.get_barrier_semaphore()

    def greet(target):
        pl.semaphore_signal(barrier, inc=1, device_id=target, device_id_type=MESH)

    @pl.loop(0, 64)
    def _(i):
        zh_, x_, c_, yy = i // 16, (i // 4) % 4, (i // 2) % 2, 2 * c + i % 2
        target = place(zh_, x_, c_, yy, zl)

        @pl.when(jnp.logical_not((zh_ == zh) & (x_ == x) & (c_ == c) & (yy == y)))
        def _():
            greet(target)

    @pl.loop(1, 16)
    def _(i):
        greet(place((zh + i // 4) % 4, (x + i % 4) % 4, c, y, zl))

    greet(place(zh, x, 1 - c, y, zl))

    @pl.loop(0, 32)
    def _(i):
        zh_, x_, zl_ = i // 8, (i // 2) % 4, i % 2

        @pl.when(jnp.logical_not((zh_ == zh) & (x_ == x) & (zl_ == zl) & (half_of_zh == c)))
        def _():
            greet(place(zh_, x_, half_of_zh, y, zl_))

    @pl.loop(1, 8)
    def _(i):
        greet((brick, (view + i) % 8))

    lane = lax.broadcasted_iota(jnp.int32, (8, 128), 1)
    for g in range(GROUPS):
        cells = est_ref[:, pl.ds(pl.multiple_of(16 * y, 16), 16), g * 128:(g + 1) * 128]
        est_t[:, g] = jnp.transpose(cells, (1, 0, 2))
        est_r[g, 0:PAD, :] = jnp.zeros((PAD, 128), F32)
        est_r[g, PAD + ROWS:, :] = jnp.zeros((PAD, 128), F32)
        for w in range(2):
            ratio[w, g, 0:PAD, :] = jnp.zeros((PAD, 128), F32)
            ratio[w, g, PAD + ROWS:, :] = jnp.zeros((PAD, 128), F32)
    for k in range(4):
        kern = index_ref[0, 16 * k + zh * 4 + x]
        for a in range(2):
            for q in range(TAPS):
                meta_s[k, a * TAPS + q:a * TAPS + q + 1, :] = jnp.full((1, 128), bank_ref[0, a, kern, q], F32)
        meta_s[k, 24:META, :] = table_ref[...]

    same = (core_of_y == c).astype(jnp.int32)
    back_same = (half_of_zh == c).astype(jnp.int32)
    pl.semaphore_wait(barrier, (64 - same) + 15 + 1 + (32 - back_same) + 7)

    @pl.loop(1, 16)
    def _(i):
        zh_, x_ = (zh + i // 4) % 4, (x + i % 4) % 4
        pltpu.make_async_remote_copy(
            est_t.at[zh_ * 4 + x_], est_r.at[:, pl.ds(pl.multiple_of(PAD + 8 * brick, 8), 8), :], s_est, r_est,
            device_id=place(zh_, x_, c, y, zl), device_id_type=MESH,
        ).start()

    pltpu.make_async_copy(
        est_t.at[zh * 4 + x], est_r.at[:, pl.ds(pl.multiple_of(PAD + 8 * brick, 8), 8), :], r_est
    ).start()

    @pl.when(core_of_y == c)
    def _():
        @pl.loop(1, 4)
        def _(i):
            y_ = (y + i) % 4
            pltpu.make_async_remote_copy(
                meta_s.at[y_], meta_r.at[y % 2], s_meta, r_meta,
                device_id=place(zh, x, c, y_, zl), device_id_type=MESH,
            ).start()

    @pl.when(core_of_y == c)
    def _():
        pltpu.make_async_copy(meta_s.at[y], meta_r.at[y % 2], r_meta).start()

    upper = lane < 64
    lower = (lane // 32) % 2 == 0

    @pl.loop(0, 16)
    def _(i):
        y_, zh_ = (y + i // 4) % 4, (zh + i % 4) % 4
        quad = y_ * 4 + zh_
        start = pl.multiple_of(quad * 128, 128)
        for g in range(2):
            turned = []
            for h in range(2):
                v = [cam_ref[0, h * 8 + g * 4 + n, :, pl.ds(start, 128)].astype(F32) for n in range(4)]
                v[0], v[2] = swap_lanes(v[0], v[2], 64, upper)
                v[1], v[3] = swap_lanes(v[1], v[3], 64, upper)
                v[0], v[1] = swap_lanes(v[0], v[1], 32, lower)
                v[2], v[3] = swap_lanes(v[2], v[3], 32, lower)
                turned.append(v)
            for n in range(4):
                pair = jnp.concatenate([turned[0][n], turned[1][n]], axis=0).astype(BF16)
                cam_t[quad * 4 + n, :, g * 128:(g + 1) * 128] = pair

        @pl.loop(0, 4)
        def _(n):
            x_ = (x + n) % 4
            depth = quad * 4 + x_
            here = (y_ == y) & (zh_ == zh) & (x_ == x) & (core_of_y == c)

            @pl.when(jnp.logical_not(here))
            def _():
                pltpu.make_async_remote_copy(
                    cam_t.at[depth], cam_r.at[y % 2, brick], s_cam, r_cam,
                    device_id=place(zh_, x_, core_of_y, y_, zl), device_id_type=MESH,
                ).start()

            @pl.when(here)
            def _():
                pltpu.make_async_copy(cam_t.at[depth], cam_r.at[y % 2, brick], r_cam).start()

    pltpu.make_async_copy(est_r.at[:, 8:136, :], est_r.at[:, 8:136, :], r_est).wait()

    @pl.loop(0, 16)
    def _(i):
        rows = pl.ds(pl.multiple_of(PAD + 8 * (2 * i + c), 8), 8)
        pltpu.make_async_remote_copy(
            est_r.at[:, rows, :], est_r.at[:, rows, :], s_fwd, r_fwd,
            device_id=place(zh, x, 1 - c, y, zl), device_id_type=MESH,
        ).start()

    pltpu.make_async_copy(meta_r, meta_r, r_meta).wait()
    row_id = lax.broadcasted_iota(jnp.int32, (ROWS, 128), 0).astype(F32)
    for w in range(2):
        for q in range(2 * TAPS):
            taps[w, q] = jnp.broadcast_to(meta_r[w, q:q + 1, :], (8, 128))

        @pl.loop(0, GROUPS)
        def _(g):
            for n in range(4):
                for k in range(2):
                    starts = meta_r[w, pl.ds(24 + (g * 4 + n) * 2 + k, 1), :]
                    hit = jnp.where(row_id == starts, 1.0, 0.0).astype(BF16)
                    onehot[w, g, :, n * 256 + k * 128:n * 256 + (k + 1) * 128] = hit

    pltpu.make_async_copy(est_r.at[:, 8:136, :], est_r.at[:, 8:136, :], r_fwd).wait()

    @pl.loop(0, ROWS // 8)
    def _(i):
        row = pl.multiple_of(8 * i, 8)
        for w in range(2):
            parts = [
                row_pass(lambda s, g=g: est_r[g, pl.ds(row + (PAD + s), 8), :], lambda q: taps[w, q], False)
                for g in range(GROUPS)
            ]
            sums = column_pass(parts, lambda q: taps[w, TAPS + q], False)
            for g in range(GROUPS):
                blurred[w, g, pl.ds(row, 8), :] = sums[g]

    pltpu.make_async_copy(cam_r, cam_r, r_cam).wait()
    block_lane = lax.broadcasted_iota(jnp.int32, (ROWS, 128), 1) // 32

    @pl.loop(0, 2)
    def _(w):
        for g in range(GROUPS):
            h = g // 2
            cells = cam_r[w, :, :, (g % 2) * 128:(g % 2 + 1) * 128].astype(F32)
            cells = cells[:, h * 8:(h + 1) * 8, :].reshape(ROWS, 128)
            stack = jnp.concatenate(
                [jnp.where(block_lane == n, cells, 0.0).astype(BF16) for n in range(4)], axis=0
            )
            measured = jnp.dot(onehot[w, g], stack, preferred_element_type=F32)
            ratio[w, g, PAD:PAD + ROWS, :] = measured / blurred[w, g]

    def correct(first):
        @pl.loop(0, 16)
        def _(i):
            row = pl.multiple_of(first + 8 * i, 8)
            product = None
            for w in range(2):
                parts = [
                    row_pass(lambda s, g=g: ratio[w, g, pl.ds(row + (PAD + s), 8), :], lambda q: taps[w, q], True)
                    for g in range(GROUPS)
                ]
                sums = column_pass(parts, lambda q: taps[w, TAPS + q], True)
                product = sums if product is None else [a * b for a, b in zip(product, sums)]
            for g in range(GROUPS):
                part[g, pl.ds(row, 8), :] = product[g]

    correct((1 - c) * 128)
    theirs = part.at[:, pl.ds(pl.multiple_of((1 - c) * 128, 128), 128), :]
    half = pltpu.make_async_remote_copy(
        theirs, other, s_half, r_half, device_id=place(zh, x, 1 - c, y, zl), device_id_type=MESH
    )
    half.start()
    correct(c * 128)
    half.wait()
    mine = pl.ds(pl.multiple_of(c * 128, 128), 128)
    for g in range(GROUPS):
        other[g] = other[g] * part[g, mine, :]

    @pl.loop(0, 32)
    def _(i):
        slot, h = i // 2, i % 2
        target = 16 * c + slot
        here = (target == brick) & (h == zl)
        source = other.at[pl.ds(2 * h, 2), pl.ds(pl.multiple_of(8 * slot, 8), 8), :]

        @pl.when(jnp.logical_not(here))
        def _():
            pltpu.make_async_remote_copy(
                source, back.at[zl, zh * 4 + x], s_back, r_back,
                device_id=(target, y * 2 + h), device_id_type=MESH,
            ).start()

        @pl.when(here)
        def _():
            pltpu.make_async_copy(source, back.at[zl, zh * 4 + x], r_back).start()

    pltpu.make_async_copy(back, back, r_back).wait()
    depths = pl.ds(pl.multiple_of(16 * y, 16), 16)
    for k in range(2):
        columns = pl.ds(pl.multiple_of(zl * 256 + k * 128, 128), 128)
        both = back[0, :, k] * back[1, :, k]
        out_ref[:, depths, columns] = jnp.transpose(both, (1, 0, 2)) * est_ref[:, depths, columns]

    piece = out_ref.at[:, depths, pl.ds(pl.multiple_of(zl * 256, 256), 256)]

    @pl.loop(1, 8)
    def _(i):
        pltpu.make_async_remote_copy(
            piece, piece, s_out, r_out, device_id=(brick, (view + i) % 8), device_id_type=MESH
        ).start()

    pltpu.make_async_copy(out_ref.at[0:7], out_ref.at[0:7], r_out).wait()
    pltpu.make_async_copy(out_ref.at[0:7], out_ref.at[0:7], s_out).wait()

    sent = est_r.at[:, 8:128, :]
    pltpu.make_async_copy(sent, sent, s_est).wait()
    pltpu.make_async_copy(est_r.at[:, 8:136, :], est_r.at[:, 8:136, :], s_fwd).wait()

    @pl.when(core_of_y == c)
    def _():
        pltpu.make_async_copy(meta_s.at[0:3], meta_s.at[0:3], s_meta).wait()
        pltpu.make_async_copy(cam_t.at[0:63], cam_t.at[0:63], s_cam).wait()

    @pl.when(core_of_y != c)
    def _():
        pltpu.make_async_copy(cam_t, cam_t, s_cam).wait()

    @pl.when(half_of_zh == c)
    def _():
        pltpu.make_async_copy(back.at[0, 0:15], back.at[0, 0:15], s_back).wait()
        pltpu.make_async_copy(back.at[1], back.at[1], s_back).wait()

    @pl.when(half_of_zh != c)
    def _():
        pltpu.make_async_copy(back, back, s_back).wait()


def shards(estimate, camera_blocks, block_lists, block_offsets, psf_index, psf_bank):
    starts = block_offsets[0].reshape(32, 16).T
    table = starts[:, :, None] + jnp.arange(8, dtype=jnp.int32)[None, None, :]
    table = table.reshape(32, 128).astype(F32)
    vmem = pl.BlockSpec(memory_space=pltpu.VMEM)
    smem = pl.BlockSpec(memory_space=pltpu.SMEM)
    dma = pltpu.SemaphoreType.DMA
    return pl.pallas_call(
        kernel,
        out_shape=jax.ShapeDtypeStruct(estimate.shape, F32),
        in_specs=[vmem, vmem, vmem, smem, smem],
        out_specs=vmem,
        scratch_shapes=[
            pltpu.VMEM((64, 16, 256), BF16),
            pltpu.VMEM((2, 32, 16, 256), BF16),
            pltpu.VMEM((16, GROUPS, 8, 128), F32),
            pltpu.VMEM((GROUPS, ROWS + 2 * PAD, 128), F32),
            pltpu.VMEM((4, META, 128), F32),
            pltpu.VMEM((2, META, 128), F32),
            pltpu.VMEM((2, 2 * TAPS, 8, 128), F32),
            pltpu.VMEM((2, GROUPS, ROWS, 1024), BF16),
            pltpu.VMEM((2, GROUPS, ROWS, 128), F32),
            pltpu.VMEM((2, GROUPS, ROWS + 2 * PAD, 128), F32),
            pltpu.VMEM((GROUPS, ROWS, 128), F32),
            pltpu.VMEM((GROUPS, 128, 128), F32),
            pltpu.VMEM((2, 16, 2, 8, 128), F32),
        ] + [dma] * 14,
        compiler_params=pltpu.CompilerParams(
            collective_id=0, has_side_effects=True, vmem_limit_bytes=40 * 1024 * 1024
        ),
        cost_estimate=pl.CostEstimate(flops=600_000_000, bytes_accessed=4_000_000, transcendentals=0),
    )(estimate, camera_blocks, table, psf_index, psf_bank)


def solution(mesh):
    placed = (
        P("brick", None, None),
        P("view", "brick", None, None),
        P("view", None, None, None),
        P("view", None),
        P("view", None),
        P("view", None, None, None),
    )
    return jax.shard_map(
        shards, mesh=mesh, in_specs=placed, out_specs=P("brick", None, None), check_vma=False
    )
```

```python
import functools

import jax
import jax.numpy as jnp
from jax import lax
from jax.experimental import pallas as pl
from jax.experimental.pallas import tpu as pltpu
from jax.sharding import PartitionSpec as P

F32 = jnp.float32
BF16 = jnp.bfloat16
MESH = pl.DeviceIdType.MESH
TAPS = 9
RAD = TAPS // 2
ROWS = 256
GROUPS = 4
PAD = 8
META = 24


def column_pass(parts, tap, reverse):
    lane = lax.broadcasted_iota(jnp.int32, (8, 128), 1)
    sums = [tap(RAD) * part for part in parts]
    for shift in range(-RAD, RAD + 1):
        if shift == 0:
            continue
        weight = tap(RAD - shift if reverse else RAD + shift)
        turned = [pltpu.roll(part, (-shift) % 128, 1) for part in parts]
        keep = lane < 128 - shift if shift > 0 else lane >= -shift
        for g in range(GROUPS):
            other = g + 1 if shift > 0 else g - 1
            beside = turned[other] if 0 <= other < GROUPS else jnp.zeros((8, 128), F32)
            sums[g] = sums[g] + weight * jnp.where(keep, turned[g], beside)
    return sums


def row_pass(load, tap, reverse):
    total = None
    for shift in range(-RAD, RAD + 1):
        weight = tap(RAD - shift if reverse else RAD + shift)
        term = weight * load(shift)
        total = term if total is None else total + term
    return total


def swap_lanes(low, high, width, keep):
    new_low = jnp.where(keep, low, pltpu.roll(high, width, 1))
    new_high = jnp.where(keep, pltpu.roll(low, 128 - width, 1), high)
    return new_low, new_high


def kernel(
    est_hbm, cam_hbm, starts_hbm, index_hbm, bank_hbm, out_ref,
    est_ref, cam_ref, starts_ref, index_ref, bank_ref,
    cam_t, cam_r, est_t, est_r, meta_s, meta_r, table, taps, onehot, blurred, ratio, part, other, back,
    s_load, s_est, r_est, s_fwd, r_fwd, s_meta, r_meta, s_cam, r_cam, s_half, r_half, s_back, r_back, s_out, r_out,
):
    brick = lax.axis_index("brick")
    view = lax.axis_index("view")
    zh, x, c = brick // 8, (brick // 2) % 4, brick % 2
    y, zl = view // 2, view % 2
    over = 1 - zl
    step = 2 * zl + 3
    core_of_y = y // 2
    half_of_zh = zh // 2

    loads = [
        pltpu.make_async_copy(source, target, s_load.at[n])
        for n, (source, target) in enumerate(
            [(est_hbm, est_ref), (index_hbm, index_ref), (bank_hbm, bank_ref), (starts_hbm, starts_ref), (cam_hbm, cam_ref)]
        )
    ]
    for load in loads:
        load.start()

    def place(zh_, x_, c_, y_, zl_):
        return (zh_ * 8 + x_ * 2 + c_, y_ * 2 + zl_)

    barrier = pltpu.get_barrier_semaphore()

    def greet(target):
        pl.semaphore_signal(barrier, inc=1, device_id=target, device_id_type=MESH)

    @pl.loop(0, 64)
    def _(i):
        greet(place((zh + i // 16) % 4, (x + i // 4) % 4, (i // 2) % 2, 2 * c + i % 2, over))

    def target_of(m):
        shift = jnp.where(m == 0, 0, jnp.where(m == 3, 2, step))
        return (zh + shift) % 4, jnp.where(m % 2 == 0, zl, over)

    def source_of(m):
        shift = jnp.where(m == 2, 8 - step, jnp.where(m == 1, step, jnp.where(m == 3, 2, 0)))
        return (zh + shift) % 4, jnp.where(m % 2 == 0, zl, over)

    @pl.loop(1, 16)
    def _(i):
        zh_, zl_ = source_of(i // 4)
        greet(place(zh_, (x + i % 4) % 4, c, y, zl_))

    @pl.loop(0, 32)
    def _(i):
        zh_, x_, zl_ = i // 8, (i // 2) % 4, i % 2

        @pl.when(jnp.logical_not((zh_ == zh) & (x_ == x) & (zl_ == zl) & (half_of_zh == c)))
        def _():
            greet(place(zh_, x_, half_of_zh, y, zl_))

    partner = place(zh, x, 1 - c, y, zl)
    ahead = (brick, ((y + 1) % 4) * 2 + zl)
    behind = (brick, ((y + 3) % 4) * 2 + zl)
    across = (brick, y * 2 + over)
    for target in (partner, ahead, behind, across):
        greet(target)

    lane = lax.broadcasted_iota(jnp.int32, (8, 128), 1)
    for g in range(GROUPS):
        est_r[g, 0:PAD, :] = jnp.zeros((PAD, 128), F32)
        est_r[g, PAD + ROWS:, :] = jnp.zeros((PAD, 128), F32)
        for w in range(2):
            ratio[w, g, 0:PAD, :] = jnp.zeros((PAD, 128), F32)
            ratio[w, g, PAD + ROWS:, :] = jnp.zeros((PAD, 128), F32)
    loads[0].wait()
    for g in range(GROUPS):
        cells = est_ref[:, pl.ds(pl.multiple_of(16 * y, 16), 16), g * 128:(g + 1) * 128]
        est_t[:, g] = jnp.transpose(cells, (1, 0, 2))
    for load in loads[1:4]:
        load.wait()
    for k in range(4):
        kern = index_ref[0, 16 * k + zh * 4 + x]
        for a in range(2):
            for q in range(TAPS):
                meta_s[k, a * TAPS + q:a * TAPS + q + 1, :] = jnp.full((1, 128), bank_ref[q, a, kern], F32)
        for n in range(4):
            meta_s[k, 20 + n:21 + n, :] = starts_ref[:, n * 128:(n + 1) * 128].astype(F32)

    back_same = (half_of_zh == c).astype(jnp.int32)
    pl.semaphore_wait(barrier, 64 + 15 + (32 - back_same) + 4)
    own_rows = pl.ds(pl.multiple_of(PAD + 8 * brick, 8), 8)

    @pl.loop(0, 15)
    def _(n):
        i = 15 - n
        zh_, zl_ = target_of(i // 4)
        x_ = (x + i % 4) % 4
        pltpu.make_async_remote_copy(
            est_t.at[zh_ * 4 + x_], est_r.at[:, own_rows, :], s_est, r_est,
            device_id=place(zh_, x_, c, y, zl_), device_id_type=MESH,
        ).start()

    pltpu.make_async_copy(est_t.at[zh * 4 + x], est_r.at[:, own_rows, :], r_est).start()

    @pl.when(core_of_y == c)
    def _():
        @pl.loop(0, 4)
        def _(i):
            y_ = (y + i) % 4
            pltpu.make_async_remote_copy(
                meta_s.at[y_], meta_r.at[y % 2], s_meta, r_meta,
                device_id=place(zh, x, c, y_, over), device_id_type=MESH,
            ).start()

    loads[4].wait()
    upper = lane < 64
    lower = (lane // 32) % 2 == 0

    @pl.loop(0, 16)
    def _(i):
        y_, zh_ = (y + i // 4) % 4, (zh + i % 4) % 4
        quad = y_ * 4 + zh_
        start = pl.multiple_of(quad * 128, 128)
        for g in range(2):
            turned = []
            for h in range(2):
                v = [cam_ref[0, h * 8 + g * 4 + n, :, pl.ds(start, 128)].astype(F32) for n in range(4)]
                v[0], v[2] = swap_lanes(v[0], v[2], 64, upper)
                v[1], v[3] = swap_lanes(v[1], v[3], 64, upper)
                v[0], v[1] = swap_lanes(v[0], v[1], 32, lower)
                v[2], v[3] = swap_lanes(v[2], v[3], 32, lower)
                turned.append(v)
            for n in range(4):
                pair = jnp.concatenate([turned[0][n], turned[1][n]], axis=0).astype(BF16)
                cam_t[quad * 4 + n, :, g * 128:(g + 1) * 128] = pair

        @pl.loop(0, 4)
        def _(n):
            x_ = (x + n) % 4
            depth = quad * 4 + x_
            pltpu.make_async_remote_copy(
                cam_t.at[depth], cam_r.at[y % 2, brick], s_cam, r_cam,
                device_id=place(zh_, x_, core_of_y, y_, over), device_id_type=MESH,
            ).start()

    pltpu.make_async_copy(est_r.at[:, 8:136, :], est_r.at[:, 8:136, :], r_est).wait()

    @pl.loop(0, 16)
    def _(i):
        rows = pl.ds(pl.multiple_of(PAD + 8 * (2 * i + c), 8), 8)
        pltpu.make_async_remote_copy(
            est_r.at[:, rows, :], est_r.at[:, rows, :], s_fwd, r_fwd,
            device_id=partner, device_id_type=MESH,
        ).start()

    pltpu.make_async_copy(meta_r, meta_r, r_meta).wait()
    row_id = lax.broadcasted_iota(jnp.int32, (ROWS, 128), 0).astype(F32)
    block = lax.broadcasted_iota(jnp.int32, (16, 512), 1)
    tile = lax.broadcasted_iota(jnp.int32, (16, 512), 0)
    holder = lax.broadcasted_iota(jnp.int32, (512, 256), 0) // 16
    owner = lax.broadcasted_iota(jnp.int32, (512, 256), 1) // 8
    spread = jnp.where(holder == owner, 1.0, 0.0).astype(BF16)
    inside = (lax.broadcasted_iota(jnp.int32, (16, 256), 1) % 8).astype(F32)
    for w in range(2):
        for q in range(2 * TAPS):
            taps[w, q] = jnp.broadcast_to(meta_r[w, q:q + 1, :], (8, 128))
        starts = jnp.concatenate([meta_r[w, 20 + n:21 + n, :] for n in range(4)], axis=1)
        by_tile = jnp.where(block % 16 == tile, jnp.broadcast_to(starts, (16, 512)), 0.0).astype(BF16)
        rows_of = jnp.dot(by_tile, spread, preferred_element_type=F32) + inside
        for k in range(2):
            table[w, k] = rows_of[:, k * 128:(k + 1) * 128]

        @pl.loop(0, GROUPS)
        def _(g):
            for n in range(4):
                for k in range(2):
                    first = table[w, k, pl.ds(g * 4 + n, 1), :]
                    hit = jnp.where(row_id == first, 1.0, 0.0).astype(BF16)
                    onehot[w, g, :, n * 256 + k * 128:n * 256 + (k + 1) * 128] = hit

    pltpu.make_async_copy(est_r.at[:, 8:136, :], est_r.at[:, 8:136, :], r_fwd).wait()

    @pl.loop(0, ROWS // 8)
    def _(i):
        row = pl.multiple_of(8 * i, 8)
        for w in range(2):
            parts = [
                row_pass(lambda s, g=g: est_r[g, pl.ds(row + (PAD + s), 8), :], lambda q: taps[w, q], False)
                for g in range(GROUPS)
            ]
            sums = column_pass(parts, lambda q: taps[w, TAPS + q], False)
            for g in range(GROUPS):
                blurred[w, g, pl.ds(row, 8), :] = sums[g]

    pltpu.make_async_copy(cam_r, cam_r, r_cam).wait()
    block_lane = lax.broadcasted_iota(jnp.int32, (ROWS, 128), 1) // 32

    @pl.loop(0, 2)
    def _(w):
        for g in range(GROUPS):
            h = g // 2
            cells = cam_r[w, :, :, (g % 2) * 128:(g % 2 + 1) * 128].astype(F32)
            cells = cells[:, h * 8:(h + 1) * 8, :].reshape(ROWS, 128)
            stack = jnp.concatenate(
                [jnp.where(block_lane == n, cells, 0.0).astype(BF16) for n in range(4)], axis=0
            )
            measured = jnp.dot(onehot[w, g], stack, preferred_element_type=F32)
            ratio[w, g, PAD:PAD + ROWS, :] = measured / blurred[w, g]

    def correct(first):
        @pl.loop(0, 16)
        def _(i):
            row = pl.multiple_of(first + 8 * i, 8)
            product = None
            for w in range(2):
                parts = [
                    row_pass(lambda s, g=g: ratio[w, g, pl.ds(row + (PAD + s), 8), :], lambda q: taps[w, q], True)
                    for g in range(GROUPS)
                ]
                sums = column_pass(parts, lambda q: taps[w, TAPS + q], True)
                product = sums if product is None else [a * b for a, b in zip(product, sums)]
            for g in range(GROUPS):
                part[g, pl.ds(row, 8), :] = product[g]

    correct((1 - c) * 128)
    theirs = part.at[:, pl.ds(pl.multiple_of((1 - c) * 128, 128), 128), :]
    half = pltpu.make_async_remote_copy(
        theirs, other, s_half, r_half, device_id=partner, device_id_type=MESH
    )
    half.start()
    correct(c * 128)
    half.wait()

    @pl.loop(0, 16)
    def _(i):
        slot = (brick + i) % 16
        target = 16 * c + slot
        rows = pl.ds(pl.multiple_of(8 * slot, 8), 8)
        here_rows = pl.ds(pl.multiple_of(c * 128 + 8 * slot, 8), 8)
        other[:, rows, :] = other[:, rows, :] * part[:, here_rows, :]
        for h in range(2):
            here = (target == brick) & (h == zl)
            source = other.at[2 * h:2 * h + 2, rows, :]

            @pl.when(jnp.logical_not(here))
            def _():
                pltpu.make_async_remote_copy(
                    source, back.at[zl, zh * 4 + x], s_back, r_back,
                    device_id=(target, y * 2 + h), device_id_type=MESH,
                ).start()

            @pl.when(here)
            def _():
                pltpu.make_async_copy(source, back.at[zl, zh * 4 + x], r_back).start()

    pltpu.make_async_copy(back, back, r_back).wait()

    def region(y_, zl_, k):
        rows = pl.ds(pl.multiple_of(16 * (y_ % 4), 16), 16)
        return out_ref.at[:, rows, pl.ds(pl.multiple_of(zl_ * 256 + k * 128, 128), 128)]

    def hand_on(piece, kind, k, target):
        pltpu.make_async_remote_copy(
            piece, piece, s_out, r_out.at[kind * 2 + k], device_id=target, device_id_type=MESH
        ).start()

    def arrived(piece, kind, k):
        pltpu.make_async_copy(piece, piece, r_out.at[kind * 2 + k]).wait()

    depths = pl.ds(pl.multiple_of(16 * y, 16), 16)
    for k in range(2):
        columns = pl.ds(pl.multiple_of(zl * 256 + k * 128, 128), 128)
        both = back[0, :, k] * back[1, :, k]
        out_ref[:, depths, columns] = jnp.transpose(both, (1, 0, 2)) * est_ref[:, depths, columns]
        own = region(y, zl, k)
        hand_on(own, 2, k, across)
        hand_on(own, 0, k, ahead)
        hand_on(own, 1, k, behind)

    arrived(region(y + 3, zl, 0), 0, 0)
    hand_on(region(y + 3, zl, 0), 3, 0, ahead)
    arrived(region(y + 1, zl, 1), 1, 1)
    hand_on(region(y + 1, zl, 1), 3, 1, behind)
    for k in range(2):
        arrived(region(y, over, k), 2, k)
        hand_on(region(y, over, k), 4, k, ahead)
        hand_on(region(y, over, k), 5, k, behind)
    for k in range(2):
        arrived(region(y + 2, zl, k), 3, k)
        hand_on(region(y + 2, zl, k), 6, k, across)
    arrived(region(y + 3, zl, 1), 0, 1)
    arrived(region(y + 1, zl, 0), 1, 0)
    for k in range(2):
        arrived(region(y + 3, over, k), 4, k)
        arrived(region(y + 1, over, k), 5, k)
        arrived(region(y + 2, over, k), 6, k)

    pltpu.make_async_copy(out_ref.at[0:7], out_ref.at[0:7], s_out).wait()
    pltpu.make_async_copy(est_t.at[0:15], est_t.at[0:15], s_est).wait()
    pltpu.make_async_copy(est_r.at[:, 8:136, :], est_r.at[:, 8:136, :], s_fwd).wait()
    pltpu.make_async_copy(cam_t, cam_t, s_cam).wait()

    @pl.when(core_of_y == c)
    def _():
        pltpu.make_async_copy(meta_s, meta_s, s_meta).wait()

    @pl.when(half_of_zh == c)
    def _():
        pltpu.make_async_copy(back.at[0, 0:15], back.at[0, 0:15], s_back).wait()
        pltpu.make_async_copy(back.at[1], back.at[1], s_back).wait()

    @pl.when(half_of_zh != c)
    def _():
        pltpu.make_async_copy(back, back, s_back).wait()


def shards(estimate, camera_blocks, block_lists, block_offsets, psf_index, psf_bank):
    bank = psf_bank[0].transpose(2, 0, 1)
    hbm = pl.BlockSpec(memory_space=pltpu.HBM)
    dma = pltpu.SemaphoreType.DMA
    return pl.pallas_call(
        kernel,
        out_shape=jax.ShapeDtypeStruct(estimate.shape, F32),
        in_specs=[hbm] * 5,
        out_specs=pl.BlockSpec(memory_space=pltpu.VMEM),
        scratch_shapes=[
            pltpu.VMEM(estimate.shape, F32),
            pltpu.VMEM(camera_blocks.shape, BF16),
            pltpu.VMEM(block_offsets.shape, jnp.int32),
            pltpu.SMEM(psf_index.shape, jnp.int32),
            pltpu.SMEM(bank.shape, F32),
            pltpu.VMEM((64, 16, 256), BF16),
            pltpu.VMEM((2, 32, 16, 256), BF16),
            pltpu.VMEM((16, GROUPS, 8, 128), F32),
            pltpu.VMEM((GROUPS, ROWS + 2 * PAD, 128), F32),
            pltpu.VMEM((4, META, 128), F32),
            pltpu.VMEM((2, META, 128), F32),
            pltpu.VMEM((2, 2, 16, 128), F32),
            pltpu.VMEM((2, 2 * TAPS, 8, 128), F32),
            pltpu.VMEM((2, GROUPS, ROWS, 1024), BF16),
            pltpu.VMEM((2, GROUPS, ROWS, 128), F32),
            pltpu.VMEM((2, GROUPS, ROWS + 2 * PAD, 128), F32),
            pltpu.VMEM((GROUPS, ROWS, 128), F32),
            pltpu.VMEM((GROUPS, 128, 128), F32),
            pltpu.VMEM((2, 16, 2, 8, 128), F32),
        ] + [dma((5,))] + [dma] * 13 + [dma((14,))],
        compiler_params=pltpu.CompilerParams(
            collective_id=0, has_side_effects=True, vmem_limit_bytes=56 * 1024 * 1024
        ),
        cost_estimate=pl.CostEstimate(flops=600_000_000, bytes_accessed=4_000_000, transcendentals=0),
    )(estimate, camera_blocks, block_offsets, psf_index, bank)


def solution(mesh):
    placed = (
        P("brick", None, None),
        P("view", "brick", None, None),
        P("view", None, None, None),
        P("view", None),
        P("view", None),
        P("view", None, None, None),
    )
    return jax.shard_map(
        shards, mesh=mesh, in_specs=placed, out_specs=P("brick", None, None), check_vma=False
    )
```

```python
import functools

import jax
import jax.numpy as jnp
from jax import lax
from jax.experimental import pallas as pl
from jax.experimental.pallas import tpu as pltpu
from jax.sharding import PartitionSpec as P

F32 = jnp.float32
BF16 = jnp.bfloat16
MESH = pl.DeviceIdType.MESH
TAPS = 9
RAD = TAPS // 2
ROWS = 256
GROUPS = 4
PAD = 8
META = 24
MIDDLE = 1.25
STEPS = 43688.0


def column_pass(parts, tap, reverse):
    lane = lax.broadcasted_iota(jnp.int32, (8, 128), 1)
    sums = [tap(RAD) * part for part in parts]
    for shift in range(-RAD, RAD + 1):
        if shift == 0:
            continue
        weight = tap(RAD - shift if reverse else RAD + shift)
        turned = [pltpu.roll(part, (-shift) % 128, 1) for part in parts]
        keep = lane < 128 - shift if shift > 0 else lane >= -shift
        for g in range(GROUPS):
            other = g + 1 if shift > 0 else g - 1
            beside = turned[other] if 0 <= other < GROUPS else jnp.zeros((8, 128), F32)
            sums[g] = sums[g] + weight * jnp.where(keep, turned[g], beside)
    return sums


def row_pass(load, tap, reverse):
    total = None
    for shift in range(-RAD, RAD + 1):
        weight = tap(RAD - shift if reverse else RAD + shift)
        term = weight * load(shift)
        total = term if total is None else total + term
    return total


def swap_lanes(low, high, width, keep):
    new_low = jnp.where(keep, low, pltpu.roll(high, width, 1))
    new_high = jnp.where(keep, pltpu.roll(low, 128 - width, 1), high)
    return new_low, new_high


def kernel(
    est_hbm, cam_hbm, starts_hbm, index_hbm, bank_hbm, out_ref,
    est_ref, cam_ref, starts_ref, index_ref, bank_ref,
    cam_t, cam_r, est_t, est_q, est_r, meta_s, meta_r, table, taps, onehot, blurred, measured, ratio, part, other, back,
    s_load, s_est, r_est, s_fwd, r_fwd, s_meta, r_meta, s_cam, r_cam, s_half, r_half, s_back, r_back, s_out, r_out,
):
    brick = lax.axis_index("brick")
    view = lax.axis_index("view")
    zh, x, c = brick // 8, (brick // 2) % 4, brick % 2
    y, zl = view // 2, view % 2
    over = 1 - zl
    step = 2 * zl + 3
    core_of_y = y // 2
    half_of_zh = zh // 2

    loads = [
        pltpu.make_async_copy(source, target, s_load.at[n])
        for n, (source, target) in enumerate(
            [(est_hbm, est_ref), (index_hbm, index_ref), (bank_hbm, bank_ref), (starts_hbm, starts_ref), (cam_hbm, cam_ref)]
        )
    ]
    for load in loads:
        load.start()

    def place(zh_, x_, c_, y_, zl_):
        return (zh_ * 8 + x_ * 2 + c_, y_ * 2 + zl_)

    barrier = pltpu.get_barrier_semaphore()

    def greet(target):
        pl.semaphore_signal(barrier, inc=1, device_id=target, device_id_type=MESH)

    @pl.loop(0, 64)
    def _(i):
        greet(place((zh + i // 16) % 4, (x + i // 4) % 4, (i // 2) % 2, 2 * c + i % 2, over))

    def target_of(m):
        shift = jnp.where(m == 0, 0, jnp.where(m == 3, 2, step))
        return (zh + shift) % 4, jnp.where(m % 2 == 0, zl, over)

    def source_of(m):
        shift = jnp.where(m == 2, 8 - step, jnp.where(m == 1, step, jnp.where(m == 3, 2, 0)))
        return (zh + shift) % 4, jnp.where(m % 2 == 0, zl, over)

    @pl.loop(1, 16)
    def _(i):
        zh_, zl_ = source_of(i // 4)
        greet(place(zh_, (x + i % 4) % 4, c, y, zl_))

    @pl.loop(0, 32)
    def _(i):
        zh_, x_, zl_ = i // 8, (i // 2) % 4, i % 2

        @pl.when(jnp.logical_not((zh_ == zh) & (x_ == x) & (zl_ == zl) & (half_of_zh == c)))
        def _():
            greet(place(zh_, x_, half_of_zh, y, zl_))

    partner = place(zh, x, 1 - c, y, zl)
    ahead = (brick, ((y + 1) % 4) * 2 + zl)
    behind = (brick, ((y + 3) % 4) * 2 + zl)
    across = (brick, y * 2 + over)
    for target in (partner, ahead, behind, across):
        greet(target)

    lane = lax.broadcasted_iota(jnp.int32, (8, 128), 1)
    for g in range(GROUPS):
        est_r[g, 0:PAD, :] = jnp.zeros((PAD, 128), F32)
        est_r[g, PAD + ROWS:, :] = jnp.zeros((PAD, 128), F32)
        for w in range(2):
            ratio[w, g, 0:PAD, :] = jnp.zeros((PAD, 128), F32)
            ratio[w, g, PAD + ROWS:, :] = jnp.zeros((PAD, 128), F32)
    loads[0].wait()
    for g in range(2):
        halves = []
        for h in range(2):
            first = h * 256 + g * 128
            cells = est_ref[:, pl.ds(pl.multiple_of(16 * y, 16), 16), first:first + 128]
            halves.append(jnp.transpose(cells, (1, 0, 2)))
        pair = jnp.round((jnp.concatenate(halves, axis=1) - MIDDLE) * STEPS)
        est_t[:, :, g * 128:(g + 1) * 128] = pair.astype(jnp.int32).astype(jnp.int16)
    for load in loads[1:4]:
        load.wait()
    for k in range(4):
        kern = index_ref[0, 16 * k + zh * 4 + x]
        for a in range(2):
            for q in range(TAPS):
                meta_s[k, a * TAPS + q:a * TAPS + q + 1, :] = jnp.full((1, 128), bank_ref[q, a, kern], F32)
        for n in range(4):
            meta_s[k, 20 + n:21 + n, :] = starts_ref[:, n * 128:(n + 1) * 128].astype(F32)

    back_same = (half_of_zh == c).astype(jnp.int32)
    pl.semaphore_wait(barrier, 64 + 15 + (32 - back_same) + 4)
    slot_here = zh * 4 + x

    @pl.loop(0, 15)
    def _(n):
        i = 15 - n
        zh_, zl_ = target_of(i // 4)
        x_ = (x + i % 4) % 4
        pltpu.make_async_remote_copy(
            est_t.at[zh_ * 4 + x_], est_q.at[c, slot_here], s_est, r_est,
            device_id=place(zh_, x_, c, y, zl_), device_id_type=MESH,
        ).start()

    pltpu.make_async_copy(est_t.at[slot_here], est_q.at[c, slot_here], r_est).start()

    @pl.when(core_of_y == c)
    def _():
        @pl.loop(0, 4)
        def _(i):
            y_ = (y + i) % 4
            pltpu.make_async_remote_copy(
                meta_s.at[y_], meta_r.at[y % 2], s_meta, r_meta,
                device_id=place(zh, x, c, y_, over), device_id_type=MESH,
            ).start()

    loads[4].wait()
    upper = lane < 64
    lower = (lane // 32) % 2 == 0

    @pl.loop(0, 16)
    def _(i):
        m = (i // 8) * 2 + i % 2
        y_, zh_ = (y + (i // 2) % 4) % 4, (zh + 1 + zl + m) % 4
        quad = y_ * 4 + zh_
        start = pl.multiple_of(quad * 128, 128)
        for g in range(2):
            turned = []
            for h in range(2):
                v = [cam_ref[0, h * 8 + g * 4 + n, :, pl.ds(start, 128)].astype(F32) for n in range(4)]
                v[0], v[2] = swap_lanes(v[0], v[2], 64, upper)
                v[1], v[3] = swap_lanes(v[1], v[3], 64, upper)
                v[0], v[1] = swap_lanes(v[0], v[1], 32, lower)
                v[2], v[3] = swap_lanes(v[2], v[3], 32, lower)
                turned.append(v)
            for n in range(4):
                pair = jnp.concatenate([turned[0][n], turned[1][n]], axis=0).astype(BF16)
                cam_t[quad * 4 + n, :, g * 128:(g + 1) * 128] = pair

        @pl.loop(0, 4)
        def _(n):
            x_ = (x + n) % 4
            depth = quad * 4 + x_
            pltpu.make_async_remote_copy(
                cam_t.at[depth], cam_r.at[y % 2, brick], s_cam, r_cam.at[m // 2],
                device_id=place(zh_, x_, core_of_y, y_, over), device_id_type=MESH,
            ).start()

    pltpu.make_async_copy(est_q.at[c], est_q.at[c], r_est).wait()
    pltpu.make_async_remote_copy(
        est_q.at[c], est_q.at[c], s_fwd, r_fwd, device_id=partner, device_id_type=MESH
    ).start()

    pltpu.make_async_copy(meta_r, meta_r, r_meta).wait()
    row_id = lax.broadcasted_iota(jnp.int32, (ROWS, 128), 0).astype(F32)
    row = lax.broadcasted_iota(jnp.int32, (16, 512), 0)
    block = lax.broadcasted_iota(jnp.int32, (16, 512), 1)
    chosen = (block // 128 == row // 4) & ((block % 16) // 4 == row % 4)
    block_ = lax.broadcasted_iota(jnp.int32, (512, 256), 0)
    entry = lax.broadcasted_iota(jnp.int32, (512, 256), 1)
    spread = ((block_ // 16) % 8 == (entry % 64) // 8) & (block_ % 4 == entry // 64)
    spread = jnp.where(spread, 1.0, 0.0).astype(BF16)
    inside = (lax.broadcasted_iota(jnp.int32, (16, 256), 1) % 8).astype(F32)

    def plane(m):
        return (zh + zl + 6 - m) % 4

    for w in range(2):
        for q in range(2 * TAPS):
            taps[w, q] = jnp.broadcast_to(meta_r[w, q:q + 1, :], (8, 128))
        starts = jnp.concatenate([meta_r[w, 20 + n:21 + n, :] for n in range(4)], axis=1)
        by_tile = jnp.where(chosen, jnp.broadcast_to(starts, (16, 512)), 0.0).astype(BF16)
        rows_of = jnp.dot(by_tile, spread, preferred_element_type=F32) + inside
        for k in range(2):
            table[w, k] = rows_of[:, k * 128:(k + 1) * 128]

        @pl.loop(0, GROUPS)
        def _(g):
            for m in range(4):
                for k in range(2):
                    first = table[w, k, pl.ds(plane(m) * 4 + g, 1), :]
                    hit = jnp.where(row_id == first, 1.0, 0.0).astype(BF16)
                    lanes = (m % 2) * 256 + k * 128
                    onehot[w, m // 2, g, :, lanes:lanes + 128] = hit

    pltpu.make_async_copy(est_q.at[1 - c], est_q.at[1 - c], r_fwd).wait()

    @pl.loop(0, 32)
    def _(d):
        cells = est_q[d % 2, d // 2].astype(jnp.int32).astype(F32) * (1.0 / STEPS) + MIDDLE
        rows = pl.ds(pl.multiple_of(PAD + 8 * d, 8), 8)
        for g in range(GROUPS):
            h, lanes = g // 2, (g % 2) * 128
            est_r[g, rows, :] = cells[h * 8:(h + 1) * 8, lanes:lanes + 128]

    @pl.loop(0, ROWS // 8)
    def _(i):
        row = pl.multiple_of(8 * i, 8)
        for w in range(2):
            parts = [
                row_pass(lambda s, g=g: est_r[g, pl.ds(row + (PAD + s), 8), :], lambda q: taps[w, q], False)
                for g in range(GROUPS)
            ]
            sums = column_pass(parts, lambda q: taps[w, TAPS + q], False)
            for g in range(GROUPS):
                blurred[w, g, pl.ds(row, 8), :] = sums[g]

    block_lane = lax.broadcasted_iota(jnp.int32, (64, 128), 1) // 32
    for half in range(2):
        pltpu.make_async_copy(cam_r.at[half], cam_r.at[half], r_cam.at[half]).wait()

        @pl.loop(0, 2)
        def _(w):
            for g in range(GROUPS):
                h = g // 2
                stack = []
                for m in (2 * half, 2 * half + 1):
                    holders = pl.ds(pl.multiple_of(plane(m) * 8, 8), 8)
                    cells = cam_r[w, holders, :, (g % 2) * 128:(g % 2 + 1) * 128].astype(F32)
                    cells = cells[:, h * 8:(h + 1) * 8, :].reshape(64, 128)
                    stack += [jnp.where(block_lane == n, cells, 0.0).astype(BF16) for n in range(4)]
                landed = jnp.dot(
                    onehot[w, half, g], jnp.concatenate(stack, axis=0), preferred_element_type=F32
                )
                if half == 0:
                    measured[w, g] = landed
                else:
                    ratio[w, g, PAD:PAD + ROWS, :] = (measured[w, g] + landed) / blurred[w, g]

    def correct(first):
        @pl.loop(0, 16)
        def _(i):
            row = pl.multiple_of(first + 8 * i, 8)
            product = None
            for w in range(2):
                parts = [
                    row_pass(lambda s, g=g: ratio[w, g, pl.ds(row + (PAD + s), 8), :], lambda q: taps[w, q], True)
                    for g in range(GROUPS)
                ]
                sums = column_pass(parts, lambda q: taps[w, TAPS + q], True)
                product = sums if product is None else [a * b for a, b in zip(product, sums)]
            for g in range(GROUPS):
                part[g, pl.ds(row, 8), :] = product[g]

    correct((1 - c) * 128)
    theirs = part.at[:, pl.ds(pl.multiple_of((1 - c) * 128, 128), 128), :]
    swap = pltpu.make_async_remote_copy(
        theirs, other, s_half, r_half, device_id=partner, device_id_type=MESH
    )
    swap.start()
    correct(c * 128)
    swap.wait()

    for k in range(2):
        @pl.loop(0, 16)
        def _(i):
            slot = (brick + i) % 16
            target = 16 * c + slot
            rows = pl.ds(pl.multiple_of(8 * slot, 8), 8)
            here_rows = pl.ds(pl.multiple_of(c * 128 + 8 * slot, 8), 8)
            for h in range(2):
                here = (target == brick) & (h == zl)
                other[2 * h + k, rows, :] = other[2 * h + k, rows, :] * part[2 * h + k, here_rows, :]
                source, landing = other.at[2 * h + k, rows, :], back.at[k, zl, slot_here]

                @pl.when(jnp.logical_not(here))
                def _():
                    pltpu.make_async_remote_copy(
                        source, landing, s_back, r_back.at[k],
                        device_id=(target, y * 2 + h), device_id_type=MESH,
                    ).start()

                @pl.when(here)
                def _():
                    pltpu.make_async_copy(source, landing, r_back.at[k]).start()

    def region(y_, zl_, k):
        rows = pl.ds(pl.multiple_of(16 * (y_ % 4), 16), 16)
        return out_ref.at[:, rows, pl.ds(pl.multiple_of(zl_ * 256 + k * 128, 128), 128)]

    def hand_on(piece, kind, k, target):
        pltpu.make_async_remote_copy(
            piece, piece, s_out, r_out.at[kind * 2 + k], device_id=target, device_id_type=MESH
        ).start()

    def arrived(piece, kind, k):
        pltpu.make_async_copy(piece, piece, r_out.at[kind * 2 + k]).wait()

    depths = pl.ds(pl.multiple_of(16 * y, 16), 16)
    for k in range(2):
        columns = pl.ds(pl.multiple_of(zl * 256 + k * 128, 128), 128)
        pltpu.make_async_copy(back.at[k], back.at[k], r_back.at[k]).wait()
        both = back[k, 0] * back[k, 1]
        out_ref[:, depths, columns] = jnp.transpose(both, (1, 0, 2)) * est_ref[:, depths, columns]
        own = region(y, zl, k)
        hand_on(own, 2, k, across)
        hand_on(own, 0, k, ahead)
        hand_on(own, 1, k, behind)

    arrived(region(y + 3, zl, 0), 0, 0)
    hand_on(region(y + 3, zl, 0), 3, 0, ahead)
    arrived(region(y + 1, zl, 1), 1, 1)
    hand_on(region(y + 1, zl, 1), 3, 1, behind)
    for k in range(2):
        arrived(region(y, over, k), 2, k)
        hand_on(region(y, over, k), 4, k, ahead)
        hand_on(region(y, over, k), 5, k, behind)
    for k in range(2):
        arrived(region(y + 2, zl, k), 3, k)
        hand_on(region(y + 2, zl, k), 6, k, across)
    arrived(region(y + 3, zl, 1), 0, 1)
    arrived(region(y + 1, zl, 0), 1, 0)
    for k in range(2):
        arrived(region(y + 3, over, k), 4, k)
        arrived(region(y + 1, over, k), 5, k)
        arrived(region(y + 2, over, k), 6, k)

    pltpu.make_async_copy(out_ref.at[0:7], out_ref.at[0:7], s_out).wait()
    pltpu.make_async_copy(est_t.at[0:15], est_t.at[0:15], s_est).wait()
    pltpu.make_async_copy(est_q.at[c], est_q.at[c], s_fwd).wait()
    pltpu.make_async_copy(cam_t, cam_t, s_cam).wait()

    @pl.when(core_of_y == c)
    def _():
        pltpu.make_async_copy(meta_s, meta_s, s_meta).wait()

    @pl.when(half_of_zh == c)
    def _():
        pltpu.make_async_copy(back.at[0], back.at[0], s_back).wait()
        pltpu.make_async_copy(back.at[1, 0], back.at[1, 0], s_back).wait()
        pltpu.make_async_copy(back.at[1, 1, 0:14], back.at[1, 1, 0:14], s_back).wait()

    @pl.when(half_of_zh != c)
    def _():
        pltpu.make_async_copy(back, back, s_back).wait()


def shards(estimate, camera_blocks, block_lists, block_offsets, psf_index, psf_bank):
    bank = psf_bank[0].transpose(2, 0, 1)
    hbm = pl.BlockSpec(memory_space=pltpu.HBM)
    dma = pltpu.SemaphoreType.DMA
    return pl.pallas_call(
        kernel,
        out_shape=jax.ShapeDtypeStruct(estimate.shape, F32),
        in_specs=[hbm] * 5,
        out_specs=pl.BlockSpec(memory_space=pltpu.VMEM),
        scratch_shapes=[
            pltpu.VMEM(estimate.shape, F32),
            pltpu.VMEM(camera_blocks.shape, BF16),
            pltpu.VMEM(block_offsets.shape, jnp.int32),
            pltpu.SMEM(psf_index.shape, jnp.int32),
            pltpu.SMEM(bank.shape, F32),
            pltpu.VMEM((64, 16, 256), BF16),
            pltpu.VMEM((2, 32, 16, 256), BF16),
            pltpu.VMEM((16, 16, 256), jnp.int16),
            pltpu.VMEM((2, 16, 16, 256), jnp.int16),
            pltpu.VMEM((GROUPS, ROWS + 2 * PAD, 128), F32),
            pltpu.VMEM((4, META, 128), F32),
            pltpu.VMEM((2, META, 128), F32),
            pltpu.VMEM((2, 2, 16, 128), F32),
            pltpu.VMEM((2, 2 * TAPS, 8, 128), F32),
            pltpu.VMEM((2, 2, GROUPS, ROWS, 512), BF16),
            pltpu.VMEM((2, GROUPS, ROWS, 128), F32),
            pltpu.VMEM((2, GROUPS, ROWS, 128), F32),
            pltpu.VMEM((2, GROUPS, ROWS + 2 * PAD, 128), F32),
            pltpu.VMEM((GROUPS, ROWS, 128), F32),
            pltpu.VMEM((GROUPS, 128, 128), F32),
            pltpu.VMEM((2, 2, 16, 8, 128), F32),
        ] + [dma((5,))] + [dma] * 7 + [dma((2,))] + [dma] * 3 + [dma((2,)), dma, dma((14,))],
        compiler_params=pltpu.CompilerParams(
            collective_id=0, has_side_effects=True, vmem_limit_bytes=40 * 1024 * 1024
        ),
        cost_estimate=pl.CostEstimate(flops=600_000_000, bytes_accessed=4_000_000, transcendentals=0),
    )(*[pltpu.with_memory_space_constraint(a, pltpu.HBM) for a in (estimate, camera_blocks, block_offsets, psf_index, bank)])


def solution(mesh):
    placed = (
        P("brick", None, None),
        P("view", "brick", None, None),
        P("view", None, None, None),
        P("view", None),
        P("view", None),
        P("view", None, None, None),
    )
    return jax.shard_map(
        shards, mesh=mesh, in_specs=placed, out_specs=P("brick", None, None), check_vma=False
    )
```

```python
import functools

import jax
import jax.numpy as jnp
from jax import lax
from jax.experimental import pallas as pl
from jax.experimental.pallas import tpu as pltpu
from jax.sharding import PartitionSpec as P

F32 = jnp.float32
BF16 = jnp.bfloat16
MESH = pl.DeviceIdType.MESH
TAPS = 9
RAD = TAPS // 2
ROWS = 256
GROUPS = 4
PAD = 8
META = 24
MIDDLE = 1.25
STEPS = 43688.0


def column_pass(parts, tap, reverse):
    lane = lax.broadcasted_iota(jnp.int32, (8, 128), 1)
    sums = [tap(RAD) * part for part in parts]
    for shift in range(-RAD, RAD + 1):
        if shift == 0:
            continue
        weight = tap(RAD - shift if reverse else RAD + shift)
        turned = [pltpu.roll(part, (-shift) % 128, 1) for part in parts]
        keep = lane < 128 - shift if shift > 0 else lane >= -shift
        for g in range(GROUPS):
            other = g + 1 if shift > 0 else g - 1
            beside = turned[other] if 0 <= other < GROUPS else jnp.zeros((8, 128), F32)
            sums[g] = sums[g] + weight * jnp.where(keep, turned[g], beside)
    return sums


def row_pass(load, tap, reverse):
    total = None
    for shift in range(-RAD, RAD + 1):
        weight = tap(RAD - shift if reverse else RAD + shift)
        term = weight * load(shift)
        total = term if total is None else total + term
    return total


def swap_lanes(low, high, width, keep):
    new_low = jnp.where(keep, low, pltpu.roll(high, width, 1))
    new_high = jnp.where(keep, pltpu.roll(low, 128 - width, 1), high)
    return new_low, new_high


def kernel(
    est_hbm, cam_hbm, starts_hbm, index_hbm, bank_hbm, out_ref,
    est_ref, cam_ref, starts_ref, index_ref, bank_ref,
    cam_t, cam_r, est_t, est_q, est_r, meta_s, meta_r, table, taps, onehot, blurred, ratio, part, other, back,
    s_load, s_est, r_est, s_fwd, r_fwd, s_meta, r_meta, s_cam, r_cam, s_half, r_half, s_back, r_back, s_out, r_out,
):
    brick = lax.axis_index("brick")
    view = lax.axis_index("view")
    zh, x, c = brick // 8, (brick // 2) % 4, brick % 2
    y, zl = view // 2, view % 2
    over = 1 - zl
    step = 2 * zl + 3
    core_of_y = y // 2
    half_of_zh = zh // 2

    loads = [
        pltpu.make_async_copy(source, target, s_load.at[n])
        for n, (source, target) in enumerate(
            [(est_hbm, est_ref), (index_hbm, index_ref), (bank_hbm, bank_ref), (starts_hbm, starts_ref), (cam_hbm, cam_ref)]
        )
    ]
    for load in loads:
        load.start()

    def place(zh_, x_, c_, y_, zl_):
        return (zh_ * 8 + x_ * 2 + c_, y_ * 2 + zl_)

    barrier = pltpu.get_barrier_semaphore()

    def greet(target):
        pl.semaphore_signal(barrier, inc=1, device_id=target, device_id_type=MESH)

    @pl.loop(0, 64)
    def _(i):
        greet(place((zh + i // 16) % 4, (x + i // 4) % 4, (i // 2) % 2, 2 * c + i % 2, over))

    def target_of(m):
        shift = jnp.where(m == 0, 0, jnp.where(m == 3, 2, step))
        return (zh + shift) % 4, jnp.where(m % 2 == 0, zl, over)

    def source_of(m):
        shift = jnp.where(m == 2, 8 - step, jnp.where(m == 1, step, jnp.where(m == 3, 2, 0)))
        return (zh + shift) % 4, jnp.where(m % 2 == 0, zl, over)

    @pl.loop(1, 16)
    def _(i):
        zh_, zl_ = source_of(i // 4)
        greet(place(zh_, (x + i % 4) % 4, c, y, zl_))

    @pl.loop(0, 32)
    def _(i):
        zh_, x_, zl_ = i // 8, (i // 2) % 4, i % 2

        @pl.when(jnp.logical_not((zh_ == zh) & (x_ == x) & (zl_ == zl) & (half_of_zh == c)))
        def _():
            greet(place(zh_, x_, half_of_zh, y, zl_))

    partner = place(zh, x, 1 - c, y, zl)
    ahead = (brick, ((y + 1) % 4) * 2 + zl)
    behind = (brick, ((y + 3) % 4) * 2 + zl)
    across = (brick, y * 2 + over)
    for target in (partner, ahead, behind, across):
        greet(target)

    lane = lax.broadcasted_iota(jnp.int32, (8, 128), 1)
    for g in range(GROUPS):
        est_r[g, 0:PAD, :] = jnp.zeros((PAD, 128), F32)
        est_r[g, PAD + ROWS:, :] = jnp.zeros((PAD, 128), F32)
        for w in range(2):
            ratio[w, g, 0:PAD, :] = jnp.zeros((PAD, 128), F32)
            ratio[w, g, PAD + ROWS:, :] = jnp.zeros((PAD, 128), F32)
    loads[0].wait()
    for g in range(2):
        halves = []
        for h in range(2):
            first = h * 256 + g * 128
            cells = est_ref[:, pl.ds(pl.multiple_of(16 * y, 16), 16), first:first + 128]
            halves.append(jnp.transpose(cells, (1, 0, 2)))
        pair = jnp.round((jnp.concatenate(halves, axis=1) - MIDDLE) * STEPS)
        est_t[:, :, g * 128:(g + 1) * 128] = pair.astype(jnp.int32).astype(jnp.int16)
    for load in loads[1:4]:
        load.wait()
    for k in range(4):
        kern = index_ref[0, 16 * k + zh * 4 + x]
        for a in range(2):
            for q in range(TAPS):
                meta_s[k, a * TAPS + q:a * TAPS + q + 1, :] = jnp.full((1, 128), bank_ref[q, a, kern], F32)
        for n in range(4):
            meta_s[k, 20 + n:21 + n, :] = starts_ref[:, n * 128:(n + 1) * 128].astype(F32)

    back_same = (half_of_zh == c).astype(jnp.int32)
    pl.semaphore_wait(barrier, 64 + 15 + (32 - back_same) + 4)
    slot_here = zh * 4 + x

    @pl.loop(0, 15)
    def _(n):
        i = 15 - n
        zh_, zl_ = target_of(i // 4)
        x_ = (x + i % 4) % 4
        pltpu.make_async_remote_copy(
            est_t.at[zh_ * 4 + x_], est_q.at[c, slot_here], s_est, r_est,
            device_id=place(zh_, x_, c, y, zl_), device_id_type=MESH,
        ).start()

    pltpu.make_async_copy(est_t.at[slot_here], est_q.at[c, slot_here], r_est).start()

    @pl.when(core_of_y == c)
    def _():
        @pl.loop(0, 4)
        def _(i):
            y_ = (y + i) % 4
            pltpu.make_async_remote_copy(
                meta_s.at[y_], meta_r.at[y % 2], s_meta, r_meta,
                device_id=place(zh, x, c, y_, over), device_id_type=MESH,
            ).start()

    loads[4].wait()
    upper = lane < 64
    lower = (lane // 32) % 2 == 0

    @pl.loop(0, 16)
    def _(i):
        y_, zh_ = (y + i // 4) % 4, (zh + i % 4) % 4
        quad = y_ * 4 + zh_
        start = pl.multiple_of(quad * 128, 128)
        for g in range(2):
            turned = []
            for h in range(2):
                v = [cam_ref[0, h * 8 + g * 4 + n, :, pl.ds(start, 128)].astype(F32) for n in range(4)]
                v[0], v[2] = swap_lanes(v[0], v[2], 64, upper)
                v[1], v[3] = swap_lanes(v[1], v[3], 64, upper)
                v[0], v[1] = swap_lanes(v[0], v[1], 32, lower)
                v[2], v[3] = swap_lanes(v[2], v[3], 32, lower)
                turned.append(v)
            for n in range(4):
                pair = jnp.concatenate([turned[0][n], turned[1][n]], axis=0).astype(BF16)
                cam_t[quad * 4 + n, :, g * 128:(g + 1) * 128] = pair

        @pl.loop(0, 4)
        def _(n):
            x_ = (x + n) % 4
            depth = quad * 4 + x_
            pltpu.make_async_remote_copy(
                cam_t.at[depth], cam_r.at[y % 2, brick], s_cam, r_cam.at[y % 2],
                device_id=place(zh_, x_, core_of_y, y_, over), device_id_type=MESH,
            ).start()

    pltpu.make_async_copy(est_q.at[c], est_q.at[c], r_est).wait()
    pltpu.make_async_remote_copy(
        est_q.at[c], est_q.at[c], s_fwd, r_fwd, device_id=partner, device_id_type=MESH
    ).start()

    pltpu.make_async_copy(meta_r, meta_r, r_meta).wait()
    row_id = lax.broadcasted_iota(jnp.int32, (ROWS, 128), 0).astype(F32)
    row = lax.broadcasted_iota(jnp.int32, (16, 512), 0)
    block = lax.broadcasted_iota(jnp.int32, (16, 512), 1)
    chosen = (block // 128 == row // 4) & ((block % 16) // 4 == row % 4)
    block_ = lax.broadcasted_iota(jnp.int32, (512, 256), 0)
    entry = lax.broadcasted_iota(jnp.int32, (512, 256), 1)
    spread = ((block_ // 16) % 8 == (entry % 64) // 8) & (block_ % 4 == entry // 64)
    spread = jnp.where(spread, 1.0, 0.0).astype(BF16)
    inside = (lax.broadcasted_iota(jnp.int32, (16, 256), 1) % 8).astype(F32)

    for w in range(2):
        for q in range(2 * TAPS):
            taps[w, q] = jnp.broadcast_to(meta_r[w, q:q + 1, :], (8, 128))
        starts = jnp.concatenate([meta_r[w, 20 + n:21 + n, :] for n in range(4)], axis=1)
        by_tile = jnp.where(chosen, jnp.broadcast_to(starts, (16, 512)), 0.0).astype(BF16)
        rows_of = jnp.dot(by_tile, spread, preferred_element_type=F32) + inside
        for k in range(2):
            table[w, k] = rows_of[:, k * 128:(k + 1) * 128]

        @pl.loop(0, GROUPS)
        def _(g):
            for m in range(4):
                for k in range(2):
                    first = table[w, k, pl.ds(m * 4 + g, 1), :]
                    hit = jnp.where(row_id == first, 1.0, 0.0).astype(BF16)
                    onehot[w, g, :, m * 256 + k * 128:m * 256 + (k + 1) * 128] = hit

    pltpu.make_async_copy(est_q.at[1 - c], est_q.at[1 - c], r_fwd).wait()

    @pl.loop(0, 32)
    def _(d):
        cells = est_q[d % 2, d // 2].astype(jnp.int32).astype(F32) * (1.0 / STEPS) + MIDDLE
        rows = pl.ds(pl.multiple_of(PAD + 8 * d, 8), 8)
        for g in range(GROUPS):
            h, lanes = g // 2, (g % 2) * 128
            est_r[g, rows, :] = cells[h * 8:(h + 1) * 8, lanes:lanes + 128]

    @pl.loop(0, ROWS // 16)
    def _(i):
        for n in range(2):
            row = pl.multiple_of(16 * i + 8 * n, 8)
            for w in range(2):
                parts = [
                    row_pass(lambda s, g=g: est_r[g, pl.ds(row + (PAD + s), 8), :], lambda q: taps[w, q], False)
                    for g in range(GROUPS)
                ]
                sums = column_pass(parts, lambda q: taps[w, TAPS + q], False)
                for g in range(GROUPS):
                    blurred[w, g, pl.ds(row, 8), :] = sums[g]

    block_lane = lax.broadcasted_iota(jnp.int32, (64, 128), 1) // 32

    def measure(w):
        pltpu.make_async_copy(cam_r.at[w], cam_r.at[w], r_cam.at[w]).wait()
        for g in range(GROUPS):
            h = g // 2
            stack = []
            for m in range(4):
                cells = cam_r[w, m * 8:(m + 1) * 8, :, (g % 2) * 128:(g % 2 + 1) * 128].astype(F32)
                cells = cells[:, h * 8:(h + 1) * 8, :].reshape(64, 128)
                stack += [jnp.where(block_lane == n, cells, 0.0).astype(BF16) for n in range(4)]
            measured = jnp.dot(onehot[w, g], jnp.concatenate(stack, axis=0), preferred_element_type=F32)
            ratio[w, g, PAD:PAD + ROWS, :] = measured / blurred[w, g]

    def correct(w, first, rows, join):
        @pl.loop(0, rows // 16)
        def _(i):
            for n in range(2):
                row = pl.multiple_of(first + 16 * i + 8 * n, 8)
                parts = [
                    row_pass(lambda s, g=g: ratio[w, g, pl.ds(row + (PAD + s), 8), :], lambda q: taps[w, q], True)
                    for g in range(GROUPS)
                ]
                sums = column_pass(parts, lambda q: taps[w, TAPS + q], True)
                for g in range(GROUPS):
                    so_far = part[g, pl.ds(row, 8), :] * sums[g] if join else sums[g]
                    part[g, pl.ds(row, 8), :] = so_far

    early = jnp.where((y - 2 * c + 4) % 4 == 0, 0, 1)
    measure(early)
    correct(early, 0, ROWS, False)
    late = 1 - early
    measure(late)
    correct(late, (1 - c) * 128, 128, True)
    theirs = part.at[:, pl.ds(pl.multiple_of((1 - c) * 128, 128), 128), :]
    swap = pltpu.make_async_remote_copy(
        theirs, other, s_half, r_half, device_id=partner, device_id_type=MESH
    )
    swap.start()
    correct(late, c * 128, 128, True)
    swap.wait()

    for k in range(2):
        @pl.loop(0, 16)
        def _(i):
            slot = (brick + i) % 16
            target = 16 * c + slot
            rows = pl.ds(pl.multiple_of(8 * slot, 8), 8)
            here_rows = pl.ds(pl.multiple_of(c * 128 + 8 * slot, 8), 8)
            for h in range(2):
                here = (target == brick) & (h == zl)
                other[2 * h + k, rows, :] = other[2 * h + k, rows, :] * part[2 * h + k, here_rows, :]
                source, landing = other.at[2 * h + k, rows, :], back.at[k, zl, slot_here]

                @pl.when(jnp.logical_not(here))
                def _():
                    pltpu.make_async_remote_copy(
                        source, landing, s_back, r_back.at[k],
                        device_id=(target, y * 2 + h), device_id_type=MESH,
                    ).start()

                @pl.when(here)
                def _():
                    pltpu.make_async_copy(source, landing, r_back.at[k]).start()

    def region(y_, zl_, k):
        rows = pl.ds(pl.multiple_of(16 * (y_ % 4), 16), 16)
        return out_ref.at[:, rows, pl.ds(pl.multiple_of(zl_ * 256 + k * 128, 128), 128)]

    def hand_on(piece, kind, k, target):
        pltpu.make_async_remote_copy(
            piece, piece, s_out, r_out.at[kind * 2 + k], device_id=target, device_id_type=MESH
        ).start()

    def arrived(piece, kind, k):
        pltpu.make_async_copy(piece, piece, r_out.at[kind * 2 + k]).wait()

    depths = pl.ds(pl.multiple_of(16 * y, 16), 16)

    def begin(k):
        pltpu.make_async_copy(back.at[k], back.at[k], r_back.at[k]).wait()
        columns = pl.ds(pl.multiple_of(zl * 256 + k * 128, 128), 128)
        both = back[k, 0] * back[k, 1]
        out_ref[:, depths, columns] = jnp.transpose(both, (1, 0, 2)) * est_ref[:, depths, columns]
        own = region(y, zl, k)
        hand_on(own, 2, k, across)
        hand_on(own, k, k, behind if k else ahead)
        hand_on(own, 1 - k, k, ahead if k else behind)

    def sideways(k):
        arrived(region(y, over, k), 2, k)
        hand_on(region(y, over, k), 4, k, ahead)
        hand_on(region(y, over, k), 5, k, behind)

    def far(k):
        arrived(region(y + 2, zl, k), 3, k)
        hand_on(region(y + 2, zl, k), 6, k, across)

    begin(0)
    arrived(region(y + 3, zl, 0), 0, 0)
    hand_on(region(y + 3, zl, 0), 3, 0, ahead)
    sideways(0)
    begin(1)
    far(0)
    arrived(region(y + 1, zl, 1), 1, 1)
    hand_on(region(y + 1, zl, 1), 3, 1, behind)
    sideways(1)
    far(1)
    arrived(region(y + 3, zl, 1), 0, 1)
    arrived(region(y + 1, zl, 0), 1, 0)
    for k in range(2):
        arrived(region(y + 3, over, k), 4, k)
        arrived(region(y + 1, over, k), 5, k)
        arrived(region(y + 2, over, k), 6, k)

    pltpu.make_async_copy(out_ref.at[0:7], out_ref.at[0:7], s_out).wait()
    pltpu.make_async_copy(est_t.at[0:15], est_t.at[0:15], s_est).wait()
    pltpu.make_async_copy(est_q.at[c], est_q.at[c], s_fwd).wait()
    pltpu.make_async_copy(cam_t, cam_t, s_cam).wait()

    @pl.when(core_of_y == c)
    def _():
        pltpu.make_async_copy(meta_s, meta_s, s_meta).wait()

    @pl.when(half_of_zh == c)
    def _():
        pltpu.make_async_copy(back.at[0], back.at[0], s_back).wait()
        pltpu.make_async_copy(back.at[1, 0], back.at[1, 0], s_back).wait()
        pltpu.make_async_copy(back.at[1, 1, 0:14], back.at[1, 1, 0:14], s_back).wait()

    @pl.when(half_of_zh != c)
    def _():
        pltpu.make_async_copy(back, back, s_back).wait()


def shards(estimate, camera_blocks, block_lists, block_offsets, psf_index, psf_bank):
    bank = psf_bank[0].transpose(2, 0, 1)
    hbm = pl.BlockSpec(memory_space=pltpu.HBM)
    dma = pltpu.SemaphoreType.DMA
    return pl.pallas_call(
        kernel,
        out_shape=jax.ShapeDtypeStruct(estimate.shape, F32),
        in_specs=[hbm] * 5,
        out_specs=pl.BlockSpec(memory_space=pltpu.VMEM),
        scratch_shapes=[
            pltpu.VMEM(estimate.shape, F32),
            pltpu.VMEM(camera_blocks.shape, BF16),
            pltpu.VMEM(block_offsets.shape, jnp.int32),
            pltpu.SMEM(psf_index.shape, jnp.int32),
            pltpu.SMEM(bank.shape, F32),
            pltpu.VMEM((64, 16, 256), BF16),
            pltpu.VMEM((2, 32, 16, 256), BF16),
            pltpu.VMEM((16, 16, 256), jnp.int16),
            pltpu.VMEM((2, 16, 16, 256), jnp.int16),
            pltpu.VMEM((GROUPS, ROWS + 2 * PAD, 128), F32),
            pltpu.VMEM((4, META, 128), F32),
            pltpu.VMEM((2, META, 128), F32),
            pltpu.VMEM((2, 2, 16, 128), F32),
            pltpu.VMEM((2, 2 * TAPS, 8, 128), F32),
            pltpu.VMEM((2, GROUPS, ROWS, 1024), BF16),
            pltpu.VMEM((2, GROUPS, ROWS, 128), F32),
            pltpu.VMEM((2, GROUPS, ROWS + 2 * PAD, 128), F32),
            pltpu.VMEM((GROUPS, ROWS, 128), F32),
            pltpu.VMEM((GROUPS, 128, 128), F32),
            pltpu.VMEM((2, 2, 16, 8, 128), F32),
        ] + [dma((5,))] + [dma] * 7 + [dma((2,))] + [dma] * 3 + [dma((2,)), dma, dma((14,))],
        compiler_params=pltpu.CompilerParams(
            collective_id=0, has_side_effects=True, vmem_limit_bytes=40 * 1024 * 1024
        ),
        cost_estimate=pl.CostEstimate(flops=600_000_000, bytes_accessed=4_000_000, transcendentals=0),
    )(*[pltpu.with_memory_space_constraint(a, pltpu.HBM) for a in (estimate, camera_blocks, block_offsets, psf_index, bank)])


def solution(mesh):
    placed = (
        P("brick", None, None),
        P("view", "brick", None, None),
        P("view", None, None, None),
        P("view", None),
        P("view", None),
        P("view", None, None, None),
    )
    return jax.shard_map(
        shards, mesh=mesh, in_specs=placed, out_specs=P("brick", None, None), check_vma=False
    )
```

```python
import functools

import jax
import jax.numpy as jnp
from jax import lax
from jax.experimental import pallas as pl
from jax.experimental.pallas import tpu as pltpu
from jax.sharding import PartitionSpec as P

F32 = jnp.float32
BF16 = jnp.bfloat16
MESH = pl.DeviceIdType.MESH
TAPS = 9
RAD = TAPS // 2
ROWS = 256
GROUPS = 4
PAD = 8
META = 24
MIDDLE = 1.25
STEPS = 43688.0


def column_pass(parts, tap, reverse):
    lane = lax.broadcasted_iota(jnp.int32, (8, 128), 1)
    sums = [tap(RAD) * part for part in parts]
    for shift in range(-RAD, RAD + 1):
        if shift == 0:
            continue
        weight = tap(RAD - shift if reverse else RAD + shift)
        turned = [pltpu.roll(part, (-shift) % 128, 1) for part in parts]
        keep = lane < 128 - shift if shift > 0 else lane >= -shift
        for g in range(GROUPS):
            other = g + 1 if shift > 0 else g - 1
            beside = turned[other] if 0 <= other < GROUPS else jnp.zeros((8, 128), F32)
            sums[g] = sums[g] + weight * jnp.where(keep, turned[g], beside)
    return sums


def row_pass(load, tap, reverse):
    total = None
    for shift in range(-RAD, RAD + 1):
        weight = tap(RAD - shift if reverse else RAD + shift)
        term = weight * load(shift)
        total = term if total is None else total + term
    return total


def swap_lanes(low, high, width, keep):
    new_low = jnp.where(keep, low, pltpu.roll(high, width, 1))
    new_high = jnp.where(keep, pltpu.roll(low, 128 - width, 1), high)
    return new_low, new_high


def kernel(
    est_hbm, cam_hbm, starts_hbm, index_hbm, bank_hbm, out_ref,
    est_ref, cam_ref, starts_ref, index_ref, bank_ref,
    cam_t, cam_r, est_t, est_q, est_r, meta_s, meta_r, table, taps, onehot, blurred, ratio, part, other, back,
    s_load, s_est, r_est, s_fwd, r_fwd, s_meta, r_meta, s_cam, r_cam, s_half, r_half, s_back, r_back, s_out, r_out,
):
    brick = lax.axis_index("brick")
    view = lax.axis_index("view")
    zh, x, c = brick // 8, (brick // 2) % 4, brick % 2
    y, zl = view // 2, view % 2
    over = 1 - zl
    step = 2 * zl + 3
    core_of_y = y // 2
    half_of_zh = zh // 2

    loads = [
        pltpu.make_async_copy(source, target, s_load.at[n])
        for n, (source, target) in enumerate(
            [(est_hbm, est_ref), (index_hbm, index_ref), (bank_hbm, bank_ref), (starts_hbm, starts_ref), (cam_hbm, cam_ref)]
        )
    ]
    for load in loads:
        load.start()

    def place(zh_, x_, c_, y_, zl_):
        return (zh_ * 8 + x_ * 2 + c_, y_ * 2 + zl_)

    barrier = pltpu.get_barrier_semaphore()

    def greet(target):
        pl.semaphore_signal(barrier, inc=1, device_id=target, device_id_type=MESH)

    @pl.loop(0, 64)
    def _(i):
        greet(place((zh + i // 16) % 4, (x + i // 4) % 4, (i // 2) % 2, 2 * c + i % 2, over))

    def target_of(m):
        shift = jnp.where(m == 0, 0, jnp.where(m == 3, 2, step))
        return (zh + shift) % 4, jnp.where(m % 2 == 0, zl, over)

    def source_of(m):
        shift = jnp.where(m == 2, 8 - step, jnp.where(m == 1, step, jnp.where(m == 3, 2, 0)))
        return (zh + shift) % 4, jnp.where(m % 2 == 0, zl, over)

    @pl.loop(1, 16)
    def _(i):
        zh_, zl_ = source_of(i // 4)
        greet(place(zh_, (x + i % 4) % 4, c, y, zl_))

    @pl.loop(0, 32)
    def _(i):
        zh_, x_, zl_ = i // 8, (i // 2) % 4, i % 2

        @pl.when(jnp.logical_not((zh_ == zh) & (x_ == x) & (zl_ == zl) & (half_of_zh == c)))
        def _():
            greet(place(zh_, x_, half_of_zh, y, zl_))

    partner = place(zh, x, 1 - c, y, zl)
    ahead = (brick, ((y + 1) % 4) * 2 + zl)
    behind = (brick, ((y + 3) % 4) * 2 + zl)
    across = (brick, y * 2 + over)
    for target in (partner, ahead, behind, across):
        greet(target)

    lane = lax.broadcasted_iota(jnp.int32, (8, 128), 1)
    for g in range(GROUPS):
        est_r[g, 0:PAD, :] = jnp.zeros((PAD, 128), F32)
        est_r[g, PAD + ROWS:, :] = jnp.zeros((PAD, 128), F32)
        for w in range(2):
            ratio[w, g, 0:PAD, :] = jnp.zeros((PAD, 128), F32)
            ratio[w, g, PAD + ROWS:, :] = jnp.zeros((PAD, 128), F32)
    loads[0].wait()
    for g in range(2):
        halves = []
        for h in range(2):
            first = h * 256 + g * 128
            cells = est_ref[:, pl.ds(pl.multiple_of(16 * y, 16), 16), first:first + 128]
            halves.append(jnp.transpose(cells, (1, 0, 2)))
        pair = jnp.round((jnp.concatenate(halves, axis=1) - MIDDLE) * STEPS)
        est_t[:, :, g * 128:(g + 1) * 128] = pair.astype(jnp.int32).astype(jnp.int16)
    for load in loads[1:4]:
        load.wait()
    for k in range(4):
        kern = index_ref[0, 16 * k + zh * 4 + x]
        for a in range(2):
            for q in range(TAPS):
                meta_s[k, a * TAPS + q:a * TAPS + q + 1, :] = jnp.full((1, 128), bank_ref[q, a, kern], F32)
        for n in range(4):
            meta_s[k, 20 + n:21 + n, :] = starts_ref[:, n * 128:(n + 1) * 128].astype(F32)

    back_same = (half_of_zh == c).astype(jnp.int32)
    pl.semaphore_wait(barrier, 64 + 15 + (32 - back_same) + 4)
    slot_here = zh * 4 + x

    @pl.loop(0, 15)
    def _(n):
        i = 15 - n
        zh_, zl_ = target_of(i // 4)
        x_ = (x + i % 4) % 4
        pltpu.make_async_remote_copy(
            est_t.at[zh_ * 4 + x_], est_q.at[c, slot_here], s_est, r_est,
            device_id=place(zh_, x_, c, y, zl_), device_id_type=MESH,
        ).start()

    pltpu.make_async_copy(est_t.at[slot_here], est_q.at[c, slot_here], r_est).start()

    @pl.when(core_of_y == c)
    def _():
        @pl.loop(0, 4)
        def _(i):
            y_ = (y + i) % 4
            pltpu.make_async_remote_copy(
                meta_s.at[y_], meta_r.at[y % 2], s_meta, r_meta,
                device_id=place(zh, x, c, y_, over), device_id_type=MESH,
            ).start()

    loads[4].wait()
    upper = lane < 64
    lower = (lane // 32) % 2 == 0

    @pl.loop(0, 16)
    def _(i):
        y_, zh_ = (y + i // 4) % 4, (zh + i % 4) % 4
        quad = y_ * 4 + zh_
        start = pl.multiple_of(quad * 128, 128)
        for g in range(2):
            turned = []
            for h in range(2):
                v = [cam_ref[0, h * 8 + g * 4 + n, :, pl.ds(start, 128)].astype(F32) for n in range(4)]
                v[0], v[2] = swap_lanes(v[0], v[2], 64, upper)
                v[1], v[3] = swap_lanes(v[1], v[3], 64, upper)
                v[0], v[1] = swap_lanes(v[0], v[1], 32, lower)
                v[2], v[3] = swap_lanes(v[2], v[3], 32, lower)
                turned.append(v)
            for n in range(4):
                pair = jnp.concatenate([turned[0][n], turned[1][n]], axis=0).astype(BF16)
                cam_t[quad * 4 + n, :, g * 128:(g + 1) * 128] = pair

        @pl.loop(0, 4)
        def _(n):
            x_ = (x + n) % 4
            depth = quad * 4 + x_
            pltpu.make_async_remote_copy(
                cam_t.at[depth], cam_r.at[y % 2, brick], s_cam, r_cam.at[y % 2],
                device_id=place(zh_, x_, core_of_y, y_, over), device_id_type=MESH,
            ).start()

    pltpu.make_async_copy(est_q.at[c], est_q.at[c], r_est).wait()
    pltpu.make_async_remote_copy(
        est_q.at[c], est_q.at[c], s_fwd, r_fwd, device_id=partner, device_id_type=MESH
    ).start()

    pltpu.make_async_copy(meta_r, meta_r, r_meta).wait()
    row_id = lax.broadcasted_iota(jnp.int32, (ROWS, 128), 0).astype(F32)
    row = lax.broadcasted_iota(jnp.int32, (16, 512), 0)
    block = lax.broadcasted_iota(jnp.int32, (16, 512), 1)
    chosen = (block // 128 == row // 4) & ((block % 16) // 4 == row % 4)
    block_ = lax.broadcasted_iota(jnp.int32, (512, 256), 0)
    entry = lax.broadcasted_iota(jnp.int32, (512, 256), 1)
    spread = ((block_ // 16) % 8 == (entry % 64) // 8) & (block_ % 4 == entry // 64)
    spread = jnp.where(spread, 1.0, 0.0).astype(BF16)
    inside = (lax.broadcasted_iota(jnp.int32, (16, 256), 1) % 8).astype(F32)

    for w in range(2):
        for q in range(2 * TAPS):
            taps[w, q] = jnp.broadcast_to(meta_r[w, q:q + 1, :], (8, 128))
        starts = jnp.concatenate([meta_r[w, 20 + n:21 + n, :] for n in range(4)], axis=1)
        by_tile = jnp.where(chosen, jnp.broadcast_to(starts, (16, 512)), 0.0).astype(BF16)
        rows_of = jnp.dot(by_tile, spread, preferred_element_type=F32) + inside
        for k in range(2):
            table[w, k] = rows_of[:, k * 128:(k + 1) * 128]

        @pl.loop(0, GROUPS)
        def _(g):
            for m in range(4):
                for k in range(2):
                    first = table[w, k, pl.ds(m * 4 + g, 1), :]
                    hit = jnp.where(row_id == first, 1.0, 0.0).astype(BF16)
                    onehot[w, g, :, m * 256 + k * 128:m * 256 + (k + 1) * 128] = hit

    pltpu.make_async_copy(est_q.at[1 - c], est_q.at[1 - c], r_fwd).wait()

    @pl.loop(0, 32)
    def _(d):
        cells = est_q[d % 2, d // 2].astype(jnp.int32).astype(F32) * (1.0 / STEPS) + MIDDLE
        rows = pl.ds(pl.multiple_of(PAD + 8 * d, 8), 8)
        for g in range(GROUPS):
            h, lanes = g // 2, (g % 2) * 128
            est_r[g, rows, :] = cells[h * 8:(h + 1) * 8, lanes:lanes + 128]

    @pl.loop(0, ROWS // 16)
    def _(i):
        for n in range(2):
            row = pl.multiple_of(16 * i + 8 * n, 8)
            for w in range(2):
                parts = [
                    row_pass(lambda s, g=g: est_r[g, pl.ds(row + (PAD + s), 8), :], lambda q: taps[w, q], False)
                    for g in range(GROUPS)
                ]
                sums = column_pass(parts, lambda q: taps[w, TAPS + q], False)
                for g in range(GROUPS):
                    blurred[w, g, pl.ds(row, 8), :] = sums[g]

    block_lane = lax.broadcasted_iota(jnp.int32, (64, 128), 1) // 32

    def measure(w):
        pltpu.make_async_copy(cam_r.at[w], cam_r.at[w], r_cam.at[w]).wait()
        for g in range(GROUPS):
            h = g // 2
            stack = []
            for m in range(4):
                cells = cam_r[w, m * 8:(m + 1) * 8, :, (g % 2) * 128:(g % 2 + 1) * 128].astype(F32)
                cells = cells[:, h * 8:(h + 1) * 8, :].reshape(64, 128)
                stack += [jnp.where(block_lane == n, cells, 0.0).astype(BF16) for n in range(4)]
            measured = jnp.dot(onehot[w, g], jnp.concatenate(stack, axis=0), preferred_element_type=F32)
            ratio[w, g, PAD:PAD + ROWS, :] = measured / blurred[w, g]

    def correct(w, first, rows, join):
        @pl.loop(0, rows // 32)
        def _(i):
            for n in range(4):
                row = pl.multiple_of(first + 32 * i + 8 * n, 8)
                parts = [
                    row_pass(lambda s, g=g: ratio[w, g, pl.ds(row + (PAD + s), 8), :], lambda q: taps[w, q], True)
                    for g in range(GROUPS)
                ]
                sums = column_pass(parts, lambda q: taps[w, TAPS + q], True)
                for g in range(GROUPS):
                    so_far = part[g, pl.ds(row, 8), :] * sums[g] if join else sums[g]
                    part[g, pl.ds(row, 8), :] = so_far

    early = jnp.where((y - 2 * c + 4) % 4 == 0, 0, 1)
    measure(early)
    correct(early, 0, ROWS, False)
    late = 1 - early
    measure(late)
    correct(late, (1 - c) * 128, 128, True)
    theirs = part.at[:, pl.ds(pl.multiple_of((1 - c) * 128, 128), 128), :]
    swap = pltpu.make_async_remote_copy(
        theirs, other, s_half, r_half, device_id=partner, device_id_type=MESH
    )
    swap.start()
    correct(late, c * 128, 128, True)
    swap.wait()

    for k in range(2):
        @pl.loop(0, 16)
        def _(i):
            slot = (brick + i) % 16
            target = 16 * c + slot
            rows = pl.ds(pl.multiple_of(8 * slot, 8), 8)
            here_rows = pl.ds(pl.multiple_of(c * 128 + 8 * slot, 8), 8)
            for h in range(2):
                here = (target == brick) & (h == zl)
                other[2 * h + k, rows, :] = other[2 * h + k, rows, :] * part[2 * h + k, here_rows, :]
                source, landing = other.at[2 * h + k, rows, :], back.at[k, zl, slot_here]

                @pl.when(jnp.logical_not(here))
                def _():
                    pltpu.make_async_remote_copy(
                        source, landing, s_back, r_back.at[k],
                        device_id=(target, y * 2 + h), device_id_type=MESH,
                    ).start()

                @pl.when(here)
                def _():
                    pltpu.make_async_copy(source, landing, r_back.at[k]).start()

    def region(y_, zl_, q):
        rows = pl.ds(pl.multiple_of(16 * (y_ % 4) + 8 * (q % 2), 8), 8)
        return out_ref.at[:, rows, pl.ds(pl.multiple_of(zl_ * 256 + q // 2 * 128, 128), 128)]

    def hand_on(piece, kind, q, target):
        pltpu.make_async_remote_copy(
            piece, piece, s_out, r_out.at[kind * 4 + q], device_id=target, device_id_type=MESH
        ).start()

    def arrived(piece, kind, q):
        pltpu.make_async_copy(piece, piece, r_out.at[kind * 4 + q]).wait()

    for k in range(2):
        pltpu.make_async_copy(back.at[k], back.at[k], r_back.at[k]).wait()
        columns = pl.ds(pl.multiple_of(zl * 256 + k * 128, 128), 128)
        for d in range(2):
            q = 2 * k + d
            depths = pl.ds(pl.multiple_of(16 * y + 8 * d, 8), 8)
            both = back[k, 0, 8 * d:8 * d + 8] * back[k, 1, 8 * d:8 * d + 8]
            out_ref[:, depths, columns] = jnp.transpose(both, (1, 0, 2)) * est_ref[:, depths, columns]
            own = region(y, zl, q)
            hand_on(own, 0, q, ahead)
            hand_on(own, 1, q, behind)
            hand_on(own, 2, q, across)

    for n in range(2):
        arrived(region(y + 3, zl, n), 0, n)
        hand_on(region(y + 3, zl, n), 3, n, ahead)
        arrived(region(y + 1, zl, 2 + n), 1, 2 + n)
        hand_on(region(y + 1, zl, 2 + n), 3, 2 + n, behind)
    for q in range(4):
        arrived(region(y, over, q), 2, q)
        hand_on(region(y, over, q), 4, q, ahead)
        hand_on(region(y, over, q), 5, q, behind)
    for q in (0, 2, 1, 3):
        arrived(region(y + 2, zl, q), 3, q)
        hand_on(region(y + 2, zl, q), 6, q, across)
    for n in range(2):
        arrived(region(y + 3, zl, 2 + n), 0, 2 + n)
        arrived(region(y + 1, zl, n), 1, n)
    for q in range(4):
        arrived(region(y + 3, over, q), 4, q)
        arrived(region(y + 1, over, q), 5, q)
        arrived(region(y + 2, over, q), 6, q)

    pltpu.make_async_copy(out_ref.at[0:7], out_ref.at[0:7], s_out).wait()
    pltpu.make_async_copy(est_t.at[0:15], est_t.at[0:15], s_est).wait()
    pltpu.make_async_copy(est_q.at[c], est_q.at[c], s_fwd).wait()
    pltpu.make_async_copy(cam_t, cam_t, s_cam).wait()

    @pl.when(core_of_y == c)
    def _():
        pltpu.make_async_copy(meta_s, meta_s, s_meta).wait()

    @pl.when(half_of_zh == c)
    def _():
        pltpu.make_async_copy(back.at[0], back.at[0], s_back).wait()
        pltpu.make_async_copy(back.at[1, 0], back.at[1, 0], s_back).wait()
        pltpu.make_async_copy(back.at[1, 1, 0:14], back.at[1, 1, 0:14], s_back).wait()

    @pl.when(half_of_zh != c)
    def _():
        pltpu.make_async_copy(back, back, s_back).wait()


def shards(estimate, camera_blocks, block_lists, block_offsets, psf_index, psf_bank):
    bank = psf_bank[0].transpose(2, 0, 1)
    hbm = pl.BlockSpec(memory_space=pltpu.HBM)
    dma = pltpu.SemaphoreType.DMA
    return pl.pallas_call(
        kernel,
        out_shape=jax.ShapeDtypeStruct(estimate.shape, F32),
        in_specs=[hbm] * 5,
        out_specs=pl.BlockSpec(memory_space=pltpu.VMEM),
        scratch_shapes=[
            pltpu.VMEM(estimate.shape, F32),
            pltpu.VMEM(camera_blocks.shape, BF16),
            pltpu.VMEM(block_offsets.shape, jnp.int32),
            pltpu.SMEM(psf_index.shape, jnp.int32),
            pltpu.SMEM(bank.shape, F32),
            pltpu.VMEM((64, 16, 256), BF16),
            pltpu.VMEM((2, 32, 16, 256), BF16),
            pltpu.VMEM((16, 16, 256), jnp.int16),
            pltpu.VMEM((2, 16, 16, 256), jnp.int16),
            pltpu.VMEM((GROUPS, ROWS + 2 * PAD, 128), F32),
            pltpu.VMEM((4, META, 128), F32),
            pltpu.VMEM((2, META, 128), F32),
            pltpu.VMEM((2, 2, 16, 128), F32),
            pltpu.VMEM((2, 2 * TAPS, 8, 128), F32),
            pltpu.VMEM((2, GROUPS, ROWS, 1024), BF16),
            pltpu.VMEM((2, GROUPS, ROWS, 128), F32),
            pltpu.VMEM((2, GROUPS, ROWS + 2 * PAD, 128), F32),
            pltpu.VMEM((GROUPS, ROWS, 128), F32),
            pltpu.VMEM((GROUPS, 128, 128), F32),
            pltpu.VMEM((2, 2, 16, 8, 128), F32),
        ] + [dma((5,))] + [dma] * 7 + [dma((2,))] + [dma] * 3 + [dma((2,)), dma, dma((28,))],
        compiler_params=pltpu.CompilerParams(
            collective_id=0, has_side_effects=True, vmem_limit_bytes=40 * 1024 * 1024
        ),
        cost_estimate=pl.CostEstimate(flops=600_000_000, bytes_accessed=4_000_000, transcendentals=0),
    )(*[pltpu.with_memory_space_constraint(a, pltpu.HBM) for a in (estimate, camera_blocks, block_offsets, psf_index, bank)])


def solution(mesh):
    placed = (
        P("brick", None, None),
        P("view", "brick", None, None),
        P("view", None, None, None),
        P("view", None),
        P("view", None),
        P("view", None, None, None),
    )
    return jax.shard_map(
        shards, mesh=mesh, in_specs=placed, out_specs=P("brick", None, None), check_vma=False
    )
```

```python
import functools

import jax
import jax.numpy as jnp
from jax import lax
from jax.experimental import pallas as pl
from jax.experimental.pallas import tpu as pltpu
from jax.sharding import PartitionSpec as P

F32 = jnp.float32
BF16 = jnp.bfloat16
MESH = pl.DeviceIdType.MESH
TAPS = 9
RAD = TAPS // 2
ROWS = 256
GROUPS = 4
PAD = 8
META = 24
MIDDLE = 1.25
STEPS = 43688.0


def column_pass(parts, tap, reverse):
    lane = lax.broadcasted_iota(jnp.int32, (8, 128), 1)
    sums = [tap(RAD) * part for part in parts]
    for shift in range(-RAD, RAD + 1):
        if shift == 0:
            continue
        weight = tap(RAD - shift if reverse else RAD + shift)
        turned = [pltpu.roll(part, (-shift) % 128, 1) for part in parts]
        keep = lane < 128 - shift if shift > 0 else lane >= -shift
        for g in range(GROUPS):
            other = g + 1 if shift > 0 else g - 1
            beside = turned[other] if 0 <= other < GROUPS else jnp.zeros((8, 128), F32)
            sums[g] = sums[g] + weight * jnp.where(keep, turned[g], beside)
    return sums


def row_pass(load, tap, reverse):
    total = None
    for shift in range(-RAD, RAD + 1):
        weight = tap(RAD - shift if reverse else RAD + shift)
        term = weight * load(shift)
        total = term if total is None else total + term
    return total


def swap_lanes(low, high, width, keep):
    new_low = jnp.where(keep, low, pltpu.roll(high, width, 1))
    new_high = jnp.where(keep, pltpu.roll(low, 128 - width, 1), high)
    return new_low, new_high


def kernel(
    est_hbm, cam_hbm, starts_hbm, index_hbm, bank_hbm, out_ref,
    est_ref, cam_ref, starts_ref, index_ref, bank_ref,
    cam_t, cam_r, est_t, est_q, est_r, meta_s, meta_r, table, taps, onehot, blurred, ratio, part, other, back,
    s_load, s_est, r_est, s_fwd, r_fwd, s_meta, r_meta, s_cam, r_cam, s_half, r_half, s_back, r_back, s_out, r_out,
):
    brick = lax.axis_index("brick")
    view = lax.axis_index("view")
    zh, x, c = brick // 8, (brick // 2) % 4, brick % 2
    y, zl = view // 2, view % 2
    over = 1 - zl
    step = 2 * zl + 3
    core_of_y = y // 2
    half_of_zh = zh // 2

    loads = [
        pltpu.make_async_copy(source, target, s_load.at[n])
        for n, (source, target) in enumerate(
            [(est_hbm, est_ref), (index_hbm, index_ref), (bank_hbm, bank_ref), (starts_hbm, starts_ref), (cam_hbm, cam_ref)]
        )
    ]
    for load in loads:
        load.start()

    def place(zh_, x_, c_, y_, zl_):
        return (zh_ * 8 + x_ * 2 + c_, y_ * 2 + zl_)

    barrier = pltpu.get_barrier_semaphore()

    def greet(target):
        pl.semaphore_signal(barrier, inc=1, device_id=target, device_id_type=MESH)

    @pl.loop(0, 64)
    def _(i):
        greet(place((zh + i // 16) % 4, (x + i // 4) % 4, (i // 2) % 2, 2 * c + i % 2, over))

    def target_of(m):
        shift = jnp.where(m == 0, 0, jnp.where(m == 3, 2, step))
        return (zh + shift) % 4, jnp.where(m % 2 == 0, zl, over)

    def source_of(m):
        shift = jnp.where(m == 2, 8 - step, jnp.where(m == 1, step, jnp.where(m == 3, 2, 0)))
        return (zh + shift) % 4, jnp.where(m % 2 == 0, zl, over)

    @pl.loop(1, 16)
    def _(i):
        zh_, zl_ = source_of(i // 4)
        greet(place(zh_, (x + i % 4) % 4, c, y, zl_))

    @pl.loop(0, 32)
    def _(i):
        zh_, x_, zl_ = i // 8, (i // 2) % 4, i % 2

        @pl.when(jnp.logical_not((zh_ == zh) & (x_ == x) & (zl_ == zl) & (half_of_zh == c)))
        def _():
            greet(place(zh_, x_, half_of_zh, y, zl_))

    partner = place(zh, x, 1 - c, y, zl)
    ahead = (brick, ((y + 1) % 4) * 2 + zl)
    behind = (brick, ((y + 3) % 4) * 2 + zl)
    across = (brick, y * 2 + over)
    for target in (partner, ahead, behind, across):
        greet(target)

    lane = lax.broadcasted_iota(jnp.int32, (8, 128), 1)
    for g in range(GROUPS):
        est_r[g, 0:PAD, :] = jnp.zeros((PAD, 128), F32)
        est_r[g, PAD + ROWS:, :] = jnp.zeros((PAD, 128), F32)
        for w in range(2):
            ratio[w, g, 0:PAD, :] = jnp.zeros((PAD, 128), F32)
            ratio[w, g, PAD + ROWS:, :] = jnp.zeros((PAD, 128), F32)
    loads[0].wait()
    for g in range(2):
        halves = []
        for h in range(2):
            first = h * 256 + g * 128
            cells = est_ref[:, pl.ds(pl.multiple_of(16 * y, 16), 16), first:first + 128]
            halves.append(jnp.transpose(cells, (1, 0, 2)))
        pair = jnp.round((jnp.concatenate(halves, axis=1) - MIDDLE) * STEPS)
        est_t[:, :, g * 128:(g + 1) * 128] = pair.astype(jnp.int32).astype(jnp.int16)
    for load in loads[1:4]:
        load.wait()
    for k in range(4):
        kern = index_ref[0, 16 * k + zh * 4 + x]
        for a in range(2):
            for q in range(TAPS):
                meta_s[k, a * TAPS + q:a * TAPS + q + 1, :] = jnp.full((1, 128), bank_ref[q, a, kern], F32)
        for n in range(4):
            meta_s[k, 20 + n:21 + n, :] = starts_ref[:, n * 128:(n + 1) * 128].astype(F32)

    back_same = (half_of_zh == c).astype(jnp.int32)
    pl.semaphore_wait(barrier, 64 + 15 + (32 - back_same) + 4)
    slot_here = zh * 4 + x

    @pl.loop(0, 15)
    def _(n):
        i = 15 - n
        zh_, zl_ = target_of(i // 4)
        x_ = (x + i % 4) % 4
        pltpu.make_async_remote_copy(
            est_t.at[zh_ * 4 + x_], est_q.at[c, slot_here], s_est, r_est,
            device_id=place(zh_, x_, c, y, zl_), device_id_type=MESH,
        ).start()

    pltpu.make_async_copy(est_t.at[slot_here], est_q.at[c, slot_here], r_est).start()

    @pl.when(core_of_y == c)
    def _():
        @pl.loop(0, 4)
        def _(i):
            y_ = (y + i) % 4
            pltpu.make_async_remote_copy(
                meta_s.at[y_], meta_r.at[y % 2], s_meta, r_meta,
                device_id=place(zh, x, c, y_, over), device_id_type=MESH,
            ).start()

    loads[4].wait()
    upper = lane < 64
    lower = (lane // 32) % 2 == 0

    @pl.loop(0, 16)
    def _(i):
        y_, zh_ = (y + i // 4) % 4, (zh + i % 4) % 4
        quad = y_ * 4 + zh_
        start = pl.multiple_of(quad * 128, 128)
        for g in range(2):
            turned = []
            for h in range(2):
                v = [cam_ref[0, h * 8 + g * 4 + n, :, pl.ds(start, 128)].astype(F32) for n in range(4)]
                v[0], v[2] = swap_lanes(v[0], v[2], 64, upper)
                v[1], v[3] = swap_lanes(v[1], v[3], 64, upper)
                v[0], v[1] = swap_lanes(v[0], v[1], 32, lower)
                v[2], v[3] = swap_lanes(v[2], v[3], 32, lower)
                turned.append(v)
            for n in range(4):
                pair = jnp.concatenate([turned[0][n], turned[1][n]], axis=0).astype(BF16)
                cam_t[quad * 4 + n, :, g * 128:(g + 1) * 128] = pair

        @pl.loop(0, 4)
        def _(n):
            x_ = (x + n) % 4
            depth = quad * 4 + x_
            pltpu.make_async_remote_copy(
                cam_t.at[depth], cam_r.at[y % 2, brick], s_cam, r_cam.at[y % 2],
                device_id=place(zh_, x_, core_of_y, y_, over), device_id_type=MESH,
            ).start()

    pltpu.make_async_copy(est_q.at[c], est_q.at[c], r_est).wait()
    pltpu.make_async_remote_copy(
        est_q.at[c], est_q.at[c], s_fwd, r_fwd, device_id=partner, device_id_type=MESH
    ).start()

    pltpu.make_async_copy(meta_r, meta_r, r_meta).wait()
    row_id = lax.broadcasted_iota(jnp.int32, (ROWS, 128), 0).astype(F32)
    row = lax.broadcasted_iota(jnp.int32, (16, 512), 0)
    block = lax.broadcasted_iota(jnp.int32, (16, 512), 1)
    chosen = (block // 128 == row // 4) & ((block % 16) // 4 == row % 4)
    block_ = lax.broadcasted_iota(jnp.int32, (512, 256), 0)
    entry = lax.broadcasted_iota(jnp.int32, (512, 256), 1)
    spread = ((block_ // 16) % 8 == (entry % 64) // 8) & (block_ % 4 == entry // 64)
    spread = jnp.where(spread, 1.0, 0.0).astype(BF16)
    inside = (lax.broadcasted_iota(jnp.int32, (16, 256), 1) % 8).astype(F32)

    for w in range(2):
        for q in range(2 * TAPS):
            taps[w, q] = jnp.broadcast_to(meta_r[w, q:q + 1, :], (8, 128))
        starts = jnp.concatenate([meta_r[w, 20 + n:21 + n, :] for n in range(4)], axis=1)
        by_tile = jnp.where(chosen, jnp.broadcast_to(starts, (16, 512)), 0.0).astype(BF16)
        rows_of = jnp.dot(by_tile, spread, preferred_element_type=F32) + inside
        for k in range(2):
            table[w, k] = rows_of[:, k * 128:(k + 1) * 128]

        @pl.loop(0, GROUPS)
        def _(g):
            for m in range(4):
                for k in range(2):
                    first = table[w, k, pl.ds(m * 4 + g, 1), :]
                    hit = jnp.where(row_id == first, 1.0, 0.0).astype(BF16)
                    onehot[w, g, :, m * 256 + k * 128:m * 256 + (k + 1) * 128] = hit

    pltpu.make_async_copy(est_q.at[1 - c], est_q.at[1 - c], r_fwd).wait()

    @pl.loop(0, 32)
    def _(d):
        cells = est_q[d % 2, d // 2].astype(jnp.int32).astype(F32) * (1.0 / STEPS) + MIDDLE
        rows = pl.ds(pl.multiple_of(PAD + 8 * d, 8), 8)
        for g in range(GROUPS):
            h, lanes = g // 2, (g % 2) * 128
            est_r[g, rows, :] = cells[h * 8:(h + 1) * 8, lanes:lanes + 128]

    @pl.loop(0, ROWS // 16)
    def _(i):
        for n in range(2):
            row = pl.multiple_of(16 * i + 8 * n, 8)
            for w in range(2):
                parts = [
                    row_pass(lambda s, g=g: est_r[g, pl.ds(row + (PAD + s), 8), :], lambda q: taps[w, q], False)
                    for g in range(GROUPS)
                ]
                sums = column_pass(parts, lambda q: taps[w, TAPS + q], False)
                for g in range(GROUPS):
                    blurred[w, g, pl.ds(row, 8), :] = sums[g]

    block_lane = lax.broadcasted_iota(jnp.int32, (64, 128), 1) // 32

    def measure(w):
        pltpu.make_async_copy(cam_r.at[w], cam_r.at[w], r_cam.at[w]).wait()
        for g in range(GROUPS):
            h = g // 2
            stack = []
            for m in range(4):
                cells = cam_r[w, m * 8:(m + 1) * 8, :, (g % 2) * 128:(g % 2 + 1) * 128].astype(F32)
                cells = cells[:, h * 8:(h + 1) * 8, :].reshape(64, 128)
                stack += [jnp.where(block_lane == n, cells, 0.0).astype(BF16) for n in range(4)]
            measured = jnp.dot(onehot[w, g], jnp.concatenate(stack, axis=0), preferred_element_type=F32)
            ratio[w, g, PAD:PAD + ROWS, :] = measured / blurred[w, g]

    def correct(w, first, rows, join):
        @pl.loop(0, rows // 64)
        def _(i):
            for n in range(8):
                row = pl.multiple_of(first + 64 * i + 8 * n, 8)
                parts = [
                    row_pass(lambda s, g=g: ratio[w, g, pl.ds(row + (PAD + s), 8), :], lambda q: taps[w, q], True)
                    for g in range(GROUPS)
                ]
                sums = column_pass(parts, lambda q: taps[w, TAPS + q], True)
                for g in range(GROUPS):
                    so_far = part[g, pl.ds(row, 8), :] * sums[g] if join else sums[g]
                    part[g, pl.ds(row, 8), :] = so_far

    early = jnp.where((y - 2 * c + 4) % 4 == 0, 0, 1)
    measure(early)
    correct(early, 0, ROWS, False)
    late = 1 - early
    measure(late)
    correct(late, (1 - c) * 128, 128, True)
    theirs = part.at[:, pl.ds(pl.multiple_of((1 - c) * 128, 128), 128), :]
    swap = pltpu.make_async_remote_copy(
        theirs, other, s_half, r_half, device_id=partner, device_id_type=MESH
    )
    swap.start()
    correct(late, c * 128, 128, True)
    swap.wait()

    for k in range(2):
        @pl.loop(0, 16)
        def _(i):
            slot = (brick + i) % 16
            target = 16 * c + slot
            rows = pl.ds(pl.multiple_of(8 * slot, 8), 8)
            here_rows = pl.ds(pl.multiple_of(c * 128 + 8 * slot, 8), 8)
            for h in range(2):
                here = (target == brick) & (h == zl)
                other[2 * h + k, rows, :] = other[2 * h + k, rows, :] * part[2 * h + k, here_rows, :]
                source, landing = other.at[2 * h + k, rows, :], back.at[k, zl, slot_here]

                @pl.when(jnp.logical_not(here))
                def _():
                    pltpu.make_async_remote_copy(
                        source, landing, s_back, r_back.at[k],
                        device_id=(target, y * 2 + h), device_id_type=MESH,
                    ).start()

                @pl.when(here)
                def _():
                    pltpu.make_async_copy(source, landing, r_back.at[k]).start()

    def region(y_, zl_, q):
        rows = pl.ds(pl.multiple_of(16 * (y_ % 4) + 8 * (q % 2), 8), 8)
        return out_ref.at[:, rows, pl.ds(pl.multiple_of(zl_ * 256 + q // 2 * 128, 128), 128)]

    def hand_on(piece, kind, q, target):
        pltpu.make_async_remote_copy(
            piece, piece, s_out, r_out.at[kind * 4 + q], device_id=target, device_id_type=MESH
        ).start()

    def arrived(piece, kind, q):
        pltpu.make_async_copy(piece, piece, r_out.at[kind * 4 + q]).wait()

    for k in range(2):
        pltpu.make_async_copy(back.at[k], back.at[k], r_back.at[k]).wait()
        columns = pl.ds(pl.multiple_of(zl * 256 + k * 128, 128), 128)
        for d in range(2):
            q = 2 * k + d
            depths = pl.ds(pl.multiple_of(16 * y + 8 * d, 8), 8)
            both = back[k, 0, 8 * d:8 * d + 8] * back[k, 1, 8 * d:8 * d + 8]
            out_ref[:, depths, columns] = jnp.transpose(both, (1, 0, 2)) * est_ref[:, depths, columns]
            own = region(y, zl, q)
            hand_on(own, 0, q, ahead)
            hand_on(own, 1, q, behind)
            hand_on(own, 2, q, across)

    for n in range(2):
        arrived(region(y + 3, zl, n), 0, n)
        hand_on(region(y + 3, zl, n), 3, n, ahead)
        arrived(region(y + 1, zl, 2 + n), 1, 2 + n)
        hand_on(region(y + 1, zl, 2 + n), 3, 2 + n, behind)
    for q in range(4):
        arrived(region(y, over, q), 2, q)
        hand_on(region(y, over, q), 4, q, ahead)
        hand_on(region(y, over, q), 5, q, behind)
    for q in (0, 2, 1, 3):
        arrived(region(y + 2, zl, q), 3, q)
        hand_on(region(y + 2, zl, q), 6, q, across)
    for n in range(2):
        arrived(region(y + 3, zl, 2 + n), 0, 2 + n)
        arrived(region(y + 1, zl, n), 1, n)
    for q in range(4):
        arrived(region(y + 3, over, q), 4, q)
        arrived(region(y + 1, over, q), 5, q)
        arrived(region(y + 2, over, q), 6, q)

    pltpu.make_async_copy(out_ref.at[0:7], out_ref.at[0:7], s_out).wait()
    pltpu.make_async_copy(est_t.at[0:15], est_t.at[0:15], s_est).wait()
    pltpu.make_async_copy(est_q.at[c], est_q.at[c], s_fwd).wait()
    pltpu.make_async_copy(cam_t, cam_t, s_cam).wait()

    @pl.when(core_of_y == c)
    def _():
        pltpu.make_async_copy(meta_s, meta_s, s_meta).wait()

    @pl.when(half_of_zh == c)
    def _():
        pltpu.make_async_copy(back.at[0], back.at[0], s_back).wait()
        pltpu.make_async_copy(back.at[1, 0], back.at[1, 0], s_back).wait()
        pltpu.make_async_copy(back.at[1, 1, 0:14], back.at[1, 1, 0:14], s_back).wait()

    @pl.when(half_of_zh != c)
    def _():
        pltpu.make_async_copy(back, back, s_back).wait()


def shards(estimate, camera_blocks, block_lists, block_offsets, psf_index, psf_bank):
    bank = psf_bank[0].transpose(2, 0, 1)
    hbm = pl.BlockSpec(memory_space=pltpu.HBM)
    dma = pltpu.SemaphoreType.DMA
    return pl.pallas_call(
        kernel,
        out_shape=jax.ShapeDtypeStruct(estimate.shape, F32),
        in_specs=[hbm] * 5,
        out_specs=pl.BlockSpec(memory_space=pltpu.VMEM),
        scratch_shapes=[
            pltpu.VMEM(estimate.shape, F32),
            pltpu.VMEM(camera_blocks.shape, BF16),
            pltpu.VMEM(block_offsets.shape, jnp.int32),
            pltpu.SMEM(psf_index.shape, jnp.int32),
            pltpu.SMEM(bank.shape, F32),
            pltpu.VMEM((64, 16, 256), BF16),
            pltpu.VMEM((2, 32, 16, 256), BF16),
            pltpu.VMEM((16, 16, 256), jnp.int16),
            pltpu.VMEM((2, 16, 16, 256), jnp.int16),
            pltpu.VMEM((GROUPS, ROWS + 2 * PAD, 128), F32),
            pltpu.VMEM((4, META, 128), F32),
            pltpu.VMEM((2, META, 128), F32),
            pltpu.VMEM((2, 2, 16, 128), F32),
            pltpu.VMEM((2, 2 * TAPS, 8, 128), F32),
            pltpu.VMEM((2, GROUPS, ROWS, 1024), BF16),
            pltpu.VMEM((2, GROUPS, ROWS, 128), F32),
            pltpu.VMEM((2, GROUPS, ROWS + 2 * PAD, 128), F32),
            pltpu.VMEM((GROUPS, ROWS, 128), F32),
            pltpu.VMEM((GROUPS, 128, 128), F32),
            pltpu.VMEM((2, 2, 16, 8, 128), F32),
        ] + [dma((5,))] + [dma] * 7 + [dma((2,))] + [dma] * 3 + [dma((2,)), dma, dma((28,))],
        compiler_params=pltpu.CompilerParams(
            collective_id=0, has_side_effects=True, vmem_limit_bytes=40 * 1024 * 1024
        ),
        cost_estimate=pl.CostEstimate(flops=600_000_000, bytes_accessed=4_000_000, transcendentals=0),
    )(*[pltpu.with_memory_space_constraint(a, pltpu.HBM) for a in (estimate, camera_blocks, block_offsets, psf_index, bank)])


def solution(mesh):
    placed = (
        P("brick", None, None),
        P("view", "brick", None, None),
        P("view", None, None, None),
        P("view", None),
        P("view", None),
        P("view", None, None, None),
    )
    return jax.shard_map(
        shards, mesh=mesh, in_specs=placed, out_specs=P("brick", None, None), check_vma=False
    )
```
